128 devices in a mesh: tm: 32 (over z, x, core), space: 4 (over y).
Axes of the slice: x: 4, y: 4, z: 4, core: 2. Of those that a mesh axis runs over, the one named last changes fastest.
Arguments:
- latents: bfloat16 [256, 256, 1536], P('tm', 'space'), may hold values from -6 to 6
- mixer_weight: bfloat16 [1536, 1792], replicated, may hold values from -0.15625 to 0.15625
- step_weight: bfloat16 [1536, 12], replicated, may hold values from -0.15625 to 0.15625
- step_bias: float32 [12], replicated, may hold values from -1 to 0.5
- decay_rate: float32 [12], replicated, may hold values from 6.1035156e-06 to 0.06, as said below
- attend_weight: bfloat16 [1536, 2304], replicated, may hold values from -0.15625 to 0.15625
- output_weight: bfloat16 [2304, 1536], replicated, may hold values from -0.125 to 0.125
Outputs:
- updated: bfloat16 [256, 256, 1536], P('tm', 'space')
The draws below stay inside these ranges and needn't reach their ends.
Inputs may be any that keep to these rules, and one draw needn't show every extreme that they name: `decay_rate`: decay rates of the heads' states.
All inputs are finite; a program needn't handle non-finite values.
Results may differ from the reference program's by a relative error of at most 0.009.
Values may be sent and summed in bfloat16 or wider, within the bound.
A program may use at most 192 MiB of HBM per device.

```python
import math
import jax
import jax.numpy as jnp
from jax import lax

D = 1536
H = 12
HP = 128
N = 128
AH = 6
BLOCK = 64
FR_DEV = 8
FRAMES = 256
POS = 256
N_TM = 32
N_SPACE = 4


def draw_decay_rate(key, part):
    key = jax.random.fold_in(key, 7)
    rank_key, slow_key, fast_key = jax.random.split(key, 3)
    ordering = jax.random.permutation(rank_key, H)
    slow_count = H // 2
    slow_rates = jnp.exp(jax.random.uniform(slow_key, (H,), jnp.float32, math.log(0.1), math.log(1.5))) / (FRAMES * BLOCK)
    fast_rates = jnp.exp(jax.random.uniform(fast_key, (H,), jnp.float32, math.log(0.02), math.log(0.06)))
    return jnp.where(ordering < slow_count, slow_rates, fast_rates)


def level_of(key, dims, shards, least, high):
    factor_of = 1.0
    for axis_at, blocks in shards:
        heights = jax.random.uniform(jax.random.fold_in(jax.random.fold_in(key, 6), axis_at), (blocks,), jnp.float32, least / len(shards), high / len(shards))
        factor_of = factor_of * jnp.repeat(jnp.exp(heights), dims[axis_at] // blocks).reshape((-1,) + (1,) * (len(dims) - 1 - axis_at))
    return factor_of


def normal_values(own_key, shape, spread, limit, shards=(), dtype=jnp.bfloat16):
    drawn = jax.random.normal(own_key, shape, jnp.float32) * spread
    if len(shards) > 0:
        drawn = level_of(own_key, shape, shards, -0.22, 0.18) * drawn
    return jnp.clip(drawn, min=-limit, max=limit).astype(dtype)


def setup_inputs(seed: int = 0) -> dict:
    seeds = jax.random.split(jax.random.key(seed), 8)
    latents = normal_values(seeds[0], (FRAMES, POS, D), 1.0, 6.0, ((0, 32), (1, 4)))
    mixer_weight = normal_values(seeds[1], (D, D + 2 * N), D ** -0.5, 0.15625)
    step_weight = normal_values(seeds[2], (D, H), D ** -0.5, 0.15625)
    step_bias = jnp.clip(jax.random.uniform(seeds[3], (H,), jnp.float32, -1.0, 0.5), -1.0, 0.5)
    decay_rate = draw_decay_rate(jax.random.fold_in(seeds[7], 71), 0)
    attend_weight = normal_values(seeds[5], (D, 3 * AH * HP), D ** -0.5, 0.15625)
    output_weight = normal_values(seeds[6], (D + AH * HP, D), (D + AH * HP) ** -0.5, 0.125)
    return dict(latents=latents, mixer_weight=mixer_weight, step_weight=step_weight, step_bias=step_bias, decay_rate=decay_rate, attend_weight=attend_weight, output_weight=output_weight)


def rounded(values):
    return lax.optimization_barrier(values.astype(jnp.bfloat16))

def qk_scale(values):
    return values * lax.rsqrt(lax.optimization_barrier(jnp.mean(values * values, axis=-1, keepdims=True)) + 1e-06)

def local_states(inputs_u, b_proj, c_proj, dt_step, decay_rate):
    span_len = dt_step.shape[0]
    log_decay = jnp.cumsum(-decay_rate[None, :] * dt_step, axis=0)
    pair_dot = jnp.dot(c_proj, b_proj.T, preferred_element_type=jnp.float32)
    log_gap = log_decay.T[:, :, None] - log_decay.T[:, None, :]
    positions = jnp.arange(span_len)
    causal = positions[:, None] >= positions[None, :]
    weights = jnp.where(causal, jnp.exp(jnp.where(causal, log_gap, 0.0)), 0.0) * pair_dot[None] * dt_step.T[:, None, :]
    weights = rounded(weights)
    local_y = jnp.einsum('hts,shp->thp', weights.astype(jnp.float32), inputs_u.astype(jnp.float32))
    span_end = log_decay[-1]
    scaled = rounded((jnp.exp(span_end[None, :] - log_decay) * dt_step)[:, :, None] * inputs_u.astype(jnp.float32))
    local_state = jnp.einsum('shp,sn->hpn', scaled.astype(jnp.float32), b_proj.astype(jnp.float32))
    return (local_y, local_state, jnp.exp(span_end), log_decay)

def reference(latents, mixer_weight, step_weight, step_bias, decay_rate, attend_weight, output_weight):
    span_rows = FR_DEV * POS
    span_len = FR_DEV * BLOCK
    attend_width = AH * HP
    span_blocks = latents.reshape(N_TM, FR_DEV, POS, D)

    def by_block(flat_rows, inner_width):
        shaped = flat_rows.reshape(FR_DEV, N_SPACE, BLOCK, inner_width)
        return shaped.transpose(1, 0, 2, 3).reshape(N_SPACE, span_len, inner_width)

    def advance(carry_in, packed):
        frames, span_id = packed
        states, last_kv = carry_in
        wide_in = frames.reshape(span_rows, D).astype(jnp.float32)
        normed = rounded(wide_in * lax.rsqrt(lax.optimization_barrier(jnp.mean(wide_in * wide_in, axis=-1, keepdims=True)) + 1e-06))
        projected = jnp.dot(normed, mixer_weight, preferred_element_type=jnp.float32)
        inputs_u = rounded(projected[:, :D])
        b_proj = rounded(projected[:, D:D + N])
        c_proj = rounded(projected[:, D + N:])
        dt_step = jax.nn.softplus(jnp.dot(normed, step_weight, preferred_element_type=jnp.float32) + step_bias)
        u_blocks = by_block(inputs_u, D).reshape(N_SPACE, span_len, H, HP)
        b_blocks = by_block(b_proj, N)
        c_blocks = by_block(c_proj, N)
        dt_blocks = by_block(dt_step, H)
        local_y, local_state, total_decay, log_decay = jax.vmap(local_states, in_axes=(0, 0, 0, 0, None))(u_blocks, b_blocks, c_blocks, dt_blocks, decay_rate)
        carried = jnp.exp(log_decay)[..., None] * jnp.einsum('btn,bhpn->bthp', c_blocks.astype(jnp.float32), states, precision=lax.Precision.HIGHEST)
        mixed_y = local_y + carried
        ssm_blocks = rounded(mixed_y * lax.rsqrt(lax.optimization_barrier(jnp.mean(mixed_y * mixed_y, axis=-1, keepdims=True)) + 1e-05))
        ssm_out = ssm_blocks.reshape(N_SPACE, FR_DEV, BLOCK, D).transpose(1, 0, 2, 3).reshape(span_rows, D)
        new_states = total_decay[..., None, None] * states + local_state
        attend = jnp.dot(normed, attend_weight, preferred_element_type=jnp.float32).reshape(span_rows, 3, AH, HP)
        queries = rounded(qk_scale(attend[:, 0])).reshape(FR_DEV, POS, AH, HP)
        keys_now = rounded(qk_scale(attend[:, 1])).reshape(FR_DEV, POS, attend_width)
        values_now = rounded(attend[:, 2]).reshape(FR_DEV, POS, attend_width)
        key_value = jnp.concatenate([keys_now, values_now], axis=-1)
        key_frames = jnp.concatenate([last_kv[None], key_value[:-1]], axis=0)
        prior_keys = key_frames[..., :attend_width].reshape(FR_DEV, POS, AH, HP)
        prior_values = key_frames[..., attend_width:].reshape(FR_DEV, POS, AH, HP)
        scores = jnp.einsum('fqhd,fkhd->fhqk', queries.astype(jnp.float32), prior_keys.astype(jnp.float32)) / math.sqrt(HP)
        powers = jnp.exp(scores)
        denominator = lax.optimization_barrier(jnp.sum(powers, axis=-1))
        numerator = jnp.einsum('fhqk,fkhd->fqhd', rounded(powers).astype(jnp.float32), prior_values.astype(jnp.float32))
        frame_ids = span_id * FR_DEV + jnp.arange(FR_DEV)
        present = (frame_ids > 0).astype(jnp.float32)
        attended = rounded(numerator / jnp.transpose(denominator, (0, 2, 1))[..., None] * present[:, None, None, None]).reshape(span_rows, attend_width)
        result = wide_in + jnp.dot(ssm_out, output_weight[:D], preferred_element_type=jnp.float32) + jnp.dot(attended, output_weight[D:], preferred_element_type=jnp.float32)
        return ((new_states, key_value[-1]), result.astype(jnp.bfloat16).reshape(FR_DEV, POS, D))
    initial = (jnp.zeros((N_SPACE, H, HP, N), jnp.float32), jnp.zeros((POS, 2 * attend_width), jnp.bfloat16))
    _, outputs = lax.scan(advance, initial, (span_blocks, jnp.arange(N_TM)))
    return outputs.reshape(FRAMES, POS, D)
```

```python
import math

import jax
import jax.numpy as jnp
from jax import lax
from jax.experimental import pallas as pl
from jax.experimental.pallas import tpu as pltpu
from jax.sharding import PartitionSpec as P

MESH = pl.DeviceIdType.MESH
BF = jnp.bfloat16
F32 = jnp.float32
EXACT = lax.Precision.HIGHEST

D = 1536
H = 12
HP = 128
N = 128
AH = 6
AW = AH * HP
FR = 8
BLK = 64
ROWS = FR * BLK
POS = 256
CH = 128
NCH = ROWS // CH
TM = 32
TILE = 256


def per_head(cols):
    rows = cols.shape[0]
    return jnp.concatenate(
        [jnp.broadcast_to(cols[:, h : h + 1], (rows, HP)) for h in range(H)], axis=1
    )


def twice(v):
    return jnp.concatenate([v, v], axis=1)


def inv_rms(x, eps):
    x = x.astype(F32)
    mean = jnp.sum(x * x, axis=-1, keepdims=True) * (1.0 / x.shape[-1])
    return jnp.broadcast_to(lax.rsqrt(mean + eps), (x.shape[0], 128))


def head_scaled(v, eps):
    halves = [v[:, :HP], v[:, HP:]]
    return jnp.concatenate([p * inv_rms(p, eps) for p in halves], axis=1)


def kernel(
    lat, wm_h, ws_h, bias_ref, rate_ref, wa_h, wo_h, out_h,
    xv, xt, wm, ws, wa, wo, u, yv, acc, ob, ssm,
    kv, qt, qe, at_send, at_recv,
    r_ref, rt_ref, la_ref, lat_t, dt_t,
    s_ref, s_k, l_bf, a_recv, t_bf, b_recv, i_ref, p_bf, c_recv, d_send, d_recv, e_send, s_in,
    ld_own, ld_a, ld_t, ld_b, ld_p, ld_c,
    load_sem, own_sem, x_ssem, x_rsem, q_ssem, q_rsem, at_ssem, at_rsem,
    a_ssem, a_rsem, b_ssem, b_rsem, c_ssem, c_rsem, d_ssem, d_rsem, e_ssem, e_rsem,
):
    t = lax.axis_index("tm")
    y = lax.axis_index("space")
    core = lax.rem(t, 2)
    x = lax.rem(lax.div(t, 2), 4)
    z = lax.div(t, 8)
    t_next = lax.rem(t + 1, TM)
    t_prev = lax.rem(t + TM - 1, TM)
    ys = [lax.rem(y + d, 4) for d in range(4)]
    mate = (t + 1 - 2 * core, y)
    xs = [lax.rem(x + d, 4) for d in range(4)]
    x_dev = [(z * 8 + xs[d] * 2 + core, y) for d in range(4)]
    z_dev = [(lax.rem(z + d, 4) * 8 + x * 2 + core, y) for d in range(4)]
    last = y == 3

    def remote(src, dst, ssem, rsem, dev):
        return pltpu.make_async_remote_copy(
            src_ref=src, dst_ref=dst, send_sem=ssem, recv_sem=rsem,
            device_id=dev, device_id_type=MESH,
        )

    loads = [
        pltpu.make_async_copy(src, dst, load_sem.at[i])
        for i, (src, dst) in enumerate([(lat, xv), (ws_h, ws), (wm_h, wm), (wa_h, wa), (wo_h, wo)])
    ]
    for i in (0, 1, 2):
        loads[i].start()

    barrier = pltpu.get_barrier_semaphore()

    def greet(dev):
        pl.semaphore_signal(barrier, inc=1, device_id=dev, device_id_type=MESH)

    for d in (1, 2, 3):
        greet((t, ys[d]))
        greet(x_dev[d])
        greet(z_dev[d])
    greet(mate)
    greet((t_prev, 3))

    @pl.when(last)
    def _():
        for k in range(4):
            greet((t_next, k))

    pl.semaphore_wait(barrier, 11 + 4 * jnp.where(last, 1, 0))

    def x_copy(i, d):
        return remote(
            lat.at[pl.ds(pl.multiple_of(128 * ys[d] + 64 * i, 64), 64), :],
            xt.at[i, pl.ds(pl.multiple_of(64 * y, 64), 64), :],
            x_ssem.at[i, d], x_rsem.at[i, d], (t, ys[d]),
        )

    def x_own(i):
        return pltpu.make_async_copy(
            lat.at[pl.ds(pl.multiple_of(128 * y + 64 * i, 64), 64), :],
            xt.at[i, pl.ds(pl.multiple_of(64 * y, 64), 64), :],
            own_sem.at[i],
        )

    for i in range(2):
        for d in (2, 1, 3):
            x_copy(i, d).start()
        x_own(i).start()
    loads[3].start()
    loads[4].start()

    loads[0].wait()

    def norm_rows(j, _):
        rs = pl.ds(pl.multiple_of(j * 64, 64), 64)
        r_ref[rs, :] = inv_rms(xv[rs, :], 1e-6)
        return 0

    lax.fori_loop(0, ROWS // 64, norm_rows, 0)
    loads[1].wait()
    loads[2].wait()

    steps = jnp.dot(xv[...], ws[...], preferred_element_type=F32)
    steps = steps * r_ref[:, :H] + bias_ref[...]
    dt = jnp.maximum(steps, 0.0) + jnp.log(1.0 + jnp.exp(-jnp.abs(steps)))
    rate = rate_ref[...]
    row_id = lax.broadcasted_iota(jnp.int32, (CH, CH), 0)
    col_id = lax.broadcasted_iota(jnp.int32, (CH, CH), 1)
    causal = row_id >= col_id
    tri = jnp.where(causal, 1.0, 0.0).astype(F32)
    eye = jnp.where(row_id == col_id, 1.0, 0.0).astype(F32)
    offs = [jnp.zeros((1, H), F32)]
    ends = []
    fe = []
    for k in range(NCH):
        dt_k = dt[k * CH : (k + 1) * CH, :]
        a_k = -rate * dt_k
        la_k = jnp.dot(tri, a_k, precision=EXACT, preferred_element_type=F32)
        la_ref[k * CH : (k + 1) * CH, :] = la_k
        lat_t[k] = lax.dot_general(
            a_k, tri, (((0,), (1,)), ((), ())), precision=EXACT, preferred_element_type=F32
        )
        dt_t[k] = lax.dot_general(
            dt_k, eye, (((0,), (1,)), ((), ())), precision=EXACT, preferred_element_type=F32
        )
        end_k = la_k[CH - 1 : CH, :]
        ends.append(end_k)
        offs.append(offs[-1] + end_k)
        fe.append(jnp.exp(end_k - la_k) * dt_k)
    ld_own[...] = jnp.zeros((8, 128), F32)
    ld_t[...] = jnp.zeros((8, 128), F32)
    ld_p[...] = jnp.zeros((8, 128), F32)
    ld_own[0:1, 0:H] = offs[NCH]

    def mix(j, _):
        cs = pl.ds(pl.multiple_of(j * TILE, TILE), TILE)
        part = jnp.dot(xv[...], wm[:, cs], preferred_element_type=F32)
        u[:, cs] = (part * twice(r_ref[...])).astype(BF)
        return 0

    lax.fori_loop(0, (D + 2 * N) // TILE, mix, 0)

    loads[3].wait()

    def q_even(j, _):
        cs = pl.ds(pl.multiple_of(j * TILE, TILE), TILE)
        rows = xv[...].reshape(4, 2, BLK, D)[:, 0].reshape(4 * BLK, D)
        scale = r_ref[...].reshape(4, 2, BLK, 128)[:, 0].reshape(4 * BLK, 128)
        part = jnp.dot(rows, wa[:, cs], preferred_element_type=F32) * twice(scale)
        qe[:, :, cs] = head_scaled(part, 1e-6).astype(BF).reshape(4, BLK, TILE)
        return 0

    lax.fori_loop(0, AW // TILE, q_even, 0)

    def q_copy(k):
        dev = (t_prev, 3) if k == 0 else (t, k - 1)
        return remote(
            qe.at[k], qt.at[1, pl.ds(pl.multiple_of(64 * y, 64), 64), :],
            q_ssem.at[k], q_rsem.at[y], dev,
        )

    def q_own(k):
        return pltpu.make_async_copy(
            qe.at[k], qt.at[1, pl.ds(pl.multiple_of(64 * y, 64), 64), :], q_rsem.at[y]
        )

    q_copy(0).start()
    for k in (1, 2, 3):

        @pl.when(y != k - 1)
        def _(k=k):
            q_copy(k).start()

        @pl.when(y == k - 1)
        def _(k=k):
            q_own(k).start()

    for k in range(NCH):
        rs = pl.ds(k * CH, CH)
        scaled = (per_head(fe[k]) * u[rs, :D].astype(F32)).astype(BF)
        add = lax.dot_general(
            u[rs, D : D + N], scaled, (((0,), (0,)), ((), ())), preferred_element_type=F32
        )
        if k == 0:
            s_k[0] = jnp.zeros((N, D), BF)
            s_ref[...] = add
        else:
            s_k[k] = s_ref[...].astype(BF)
            s_ref[...] = s_ref[...] * per_head(jnp.exp(ends[k])) + add
    l_bf[...] = s_ref[...].astype(BF)

    half = pl.ds(pl.multiple_of(64 * core, 64), 64)
    other_half = pl.ds(pl.multiple_of(64 - 64 * core, 64), 64)
    a_copies = [
        remote(l_bf.at[other_half, :], a_recv, a_ssem.at[0], a_rsem.at[0], mate),
        remote(ld_own, ld_a, a_ssem.at[1], a_rsem.at[1], mate),
    ]
    for cp in a_copies:
        cp.start()

    def diag(k, _):
        rs = pl.ds(pl.multiple_of(k * CH, CH), CH)
        cb = lax.dot_general(
            u[rs, D + N : D + 2 * N], u[rs, D : D + N], (((1,), (1,)), ((), ())),
            preferred_element_type=F32,
        )
        la_k = la_ref[rs, :]
        la_row = lat_t[k]
        dt_row = dt_t[k]
        for h in range(H):
            gap = la_k[:, h : h + 1] - la_row[h : h + 1, :]
            w = jnp.exp(jnp.where(causal, gap, -1e30)) * cb * dt_row[h : h + 1, :]
            yv[rs, h * HP : (h + 1) * HP] = jnp.dot(
                w.astype(BF), u[rs, h * HP : (h + 1) * HP], preferred_element_type=F32
            )
        return 0

    lax.fori_loop(0, 2, diag, 0)

    for cp in a_copies:
        cp.wait()
    first = core == 0
    mine = s_ref[half, :]
    theirs = a_recv[...].astype(F32)
    l0 = jnp.where(first, mine, theirs)
    l1 = jnp.where(first, theirs, mine)
    ld_mine = ld_own[0:1, 0:H]
    ld_theirs = ld_a[0:1, 0:H]
    ld0 = jnp.where(first, ld_mine, ld_theirs)
    ld1 = jnp.where(first, ld_theirs, ld_mine)
    t_bf[...] = (per_head(jnp.exp(ld1)) * l0 + l1).astype(BF)
    ld_t[0:1, 0:H] = ld0 + ld1
    b_recv[x] = t_bf[pl.ds(pl.multiple_of(16 * x, 16), 16), :]
    ld_b[x] = ld_t[...]
    b_copies = []
    for d in (1, 2, 3):
        part = t_bf.at[pl.ds(pl.multiple_of(16 * xs[d], 16), 16), :]
        b_copies.append(remote(part, b_recv.at[x], b_ssem.at[0, d], b_rsem.at[0, d], x_dev[d]))
        b_copies.append(remote(ld_t, ld_b.at[x], b_ssem.at[1, d], b_rsem.at[1, d], x_dev[d]))
    for cp in b_copies:
        cp.start()

    lax.fori_loop(2, 4, diag, 0)

    for cp in b_copies:
        cp.wait()
    run = jnp.zeros((16, D), F32)
    ld_sum = jnp.zeros((1, H), F32)
    x_offs = []
    for j in range(4):
        i_ref[j] = run
        x_offs.append(ld_sum)
        ld_j = ld_b[j][0:1, 0:H]
        run = run * per_head(jnp.exp(ld_j)) + b_recv[j].astype(F32)
        ld_sum = ld_sum + ld_j
    p_bf[...] = run.astype(BF)
    ld_p[0:1, 0:H] = ld_sum
    c_recv[z] = p_bf[...]
    ld_c[z] = ld_p[...]
    c_copies = []
    for d in (1, 2, 3):
        c_copies.append(remote(p_bf, c_recv.at[z], c_ssem.at[0, d], c_rsem.at[0, d], z_dev[d]))
        c_copies.append(remote(ld_p, ld_c.at[z], c_ssem.at[1, d], c_rsem.at[1, d], z_dev[d]))
    for cp in c_copies:
        cp.start()

    def attend_proj(i, width_from, dst, dst_from, tiles, scaled_tiles):
        def body(j, _):
            src = pl.ds(pl.multiple_of(width_from + j * TILE, TILE), TILE)
            to = pl.ds(pl.multiple_of(dst_from + j * TILE, TILE), TILE)
            part = jnp.dot(xt[i], wa[:, src], preferred_element_type=F32)
            part = part * twice(rt_ref[...])
            if scaled_tiles:
                part = head_scaled(part, 1e-6)
            dst[i, :, to] = part.astype(BF)
            return 0

        lax.fori_loop(0, tiles, body, 0)

    def norm_frame(i):
        def body(j, _):
            rs = pl.ds(pl.multiple_of(j * 64, 64), 64)
            rt_ref[rs, :] = inv_rms(xt[i, rs, :], 1e-6)
            return 0

        lax.fori_loop(0, POS // 64, body, 0)

    def frame_arrived(i):
        for d in (1, 2, 3):
            x_copy(i, d).wait_recv()
        x_own(i).wait()

    frame_arrived(0)
    norm_frame(0)
    attend_proj(0, AW, kv, 0, 3, True)
    attend_proj(0, 2 * AW, kv, AW, 3, False)

    for cp in c_copies:
        cp.wait()
    run = jnp.zeros((16, D), F32)
    for j in range(4):
        nxt = run * per_head(jnp.exp(ld_c[j][0:1, 0:H])) + c_recv[j].astype(F32)
        run = jnp.where(j < z, nxt, run)
    for j in range(4):
        d_send[j] = (run * per_head(jnp.exp(x_offs[j])) + i_ref[j]).astype(BF)
    d_recv[x] = d_send[x]
    d_copies = [
        remote(d_send.at[xs[d]], d_recv.at[x], d_ssem.at[d], d_rsem.at[d], x_dev[d])
        for d in (1, 2, 3)
    ]
    for cp in d_copies:
        cp.start()

    frame_arrived(1)
    norm_frame(1)

    for cp in d_copies:
        cp.wait()
    inc0 = d_recv[...].astype(F32).reshape(64, D)
    inc1 = per_head(jnp.exp(ld0)) * inc0 + l0
    e_send[...] = jnp.where(first, inc1, inc0).astype(BF)
    s_in[half, :] = jnp.where(first, inc0, inc1).astype(BF)
    e_copy = remote(e_send, s_in.at[half, :], e_ssem, e_rsem, mate)
    e_copy.start()

    def q_odd(j, _):
        cs = pl.ds(pl.multiple_of(j * TILE, TILE), TILE)
        part = jnp.dot(xt[1], wa[:, cs], preferred_element_type=F32) * twice(rt_ref[...])
        qt[0, :, cs] = head_scaled(part, 1e-6).astype(BF)
        return 0

    lax.fori_loop(0, 3, q_odd, 0)

    def attention(i):
        for h in range(AH):
            hs = slice(h * HP, (h + 1) * HP)
            vs = slice(AW + h * HP, AW + (h + 1) * HP)
            s = lax.dot_general(
                qt[i, :, hs], kv[i, :, hs], (((1,), (1,)), ((), ())), preferred_element_type=F32
            )
            p = jnp.exp(s * (1.0 / math.sqrt(HP)))
            total = jnp.sum(p, axis=-1, keepdims=True)
            num = jnp.dot(p.astype(BF), kv[i, :, vs], preferred_element_type=F32)
            at_send[i, :, hs] = (num / total).astype(BF)

    def at_copy(i, d):
        src = at_send.at[i, pl.ds(pl.multiple_of(64 * ys[d], 64), 64), :]
        if i == 0:
            return remote(src, at_recv.at[1, y], at_ssem.at[i, d], at_rsem.at[1, y], (t, ys[d]))
        owner = jnp.where(last, t_next, t)
        k = ys[1]
        return remote(src, at_recv.at[0, k], at_ssem.at[i, d], at_rsem.at[0, k], (owner, ys[d]))

    def at_own(i):
        src = at_send.at[i, pl.ds(pl.multiple_of(64 * y, 64), 64), :]
        if i == 0:
            return pltpu.make_async_copy(src, at_recv.at[1, y], at_rsem.at[1, y])
        return pltpu.make_async_copy(src, at_recv.at[0, ys[1]], at_rsem.at[0, ys[1]])

    attention(0)
    for d in (2, 1, 3):
        at_copy(0, d).start()
    at_own(0).start()

    attend_proj(1, AW, kv, 0, 3, True)
    attend_proj(1, 2 * AW, kv, AW, 3, False)
    for k in range(4):
        pltpu.make_async_copy(qe.at[k], qt.at[1, pl.ds(64 * k, 64), :], q_rsem.at[k]).wait()
    attention(1)
    for d in (2, 1, 3):
        at_copy(1, d).start()

    @pl.when(last)
    def _():
        at_copy(1, 0).start()

    @pl.when(jnp.logical_not(last))
    def _():
        at_own(1).start()

    e_copy.wait()
    for k in range(NCH):
        rs = pl.ds(k * CH, CH)
        state = s_k[k].astype(F32) + per_head(jnp.exp(offs[k])) * s_in[...].astype(F32)
        carried = jnp.dot(
            u[rs, D + N : D + 2 * N], state.astype(BF), preferred_element_type=F32
        )
        e_k = jnp.exp(la_ref[rs, :])
        for h in range(H):
            hs = slice(h * HP, (h + 1) * HP)
            m = yv[rs, hs] + e_k[:, h : h + 1] * carried[:, hs]
            ssm[rs, hs] = (m * inv_rms(m, 1e-5)).astype(BF)

    loads[4].wait()

    def out_ssm(j, _):
        cs = pl.ds(pl.multiple_of(j * TILE, TILE), TILE)
        part = jnp.dot(ssm[...], wo[:D, cs], preferred_element_type=F32)
        acc[:, :, :, cs] = (part + xv[:, cs].astype(F32)).reshape(4, 2, BLK, TILE)
        return 0

    lax.fori_loop(0, D // TILE, out_ssm, 0)

    out_copies = []
    for par in (1, 0):
        for k in range(4):
            pltpu.make_async_copy(at_send.at[0, pl.ds(0, 64), :], at_recv.at[par, k], at_rsem.at[par, k]).wait()
        if par == 0:

            @pl.when(t == 0)
            def _():
                at_recv[0, 0] = jnp.zeros((BLK, AW), BF)

        def out_att(j, _, par=par):
            cs = pl.ds(pl.multiple_of(j * TILE, TILE), TILE)
            rows = at_recv[par].reshape(4 * BLK, AW)
            part = jnp.dot(rows, wo[D:, cs], preferred_element_type=F32)
            ob[par, :, :, cs] = (part.reshape(4, BLK, TILE) + acc[:, par, :, cs]).astype(BF)
            return 0

        lax.fori_loop(0, D // TILE, out_att, 0)
        for k in range(4):
            cp = pltpu.make_async_copy(
                ob.at[par, k], out_h.at[pl.ds(128 * k + 64 * par, 64), :], load_sem.at[5 + 4 * par + k]
            )
            cp.start()
            out_copies.append(cp)

    for i in range(2):
        for d in (1, 2, 3):
            x_copy(i, d).wait_send()
            at_copy(i, d).wait_send()

    @pl.when(last)
    def _():
        at_copy(1, 0).wait_send()

    q_copy(0).wait_send()
    for k in (1, 2, 3):

        @pl.when(y != k - 1)
        def _(k=k):
            q_copy(k).wait_send()

    for cp in out_copies:
        cp.wait()


def on_device(latents, mixer_weight, step_weight, step_bias, decay_rate, attend_weight, output_weight):
    any_spec = pl.BlockSpec(memory_space=pl.ANY)
    vmem_spec = pl.BlockSpec(memory_space=pltpu.VMEM)
    dma = pltpu.SemaphoreType.DMA
    v = pltpu.VMEM
    scratch = [
        v((ROWS, D), BF),
        v((2, POS, D), BF),
        v((D, D + 2 * N), BF),
        v((D, H), BF),
        v((D, 3 * AW), BF),
        v((D + AW, D), BF),
        v((ROWS, D + 2 * N), BF),
        v((ROWS, D), F32),
        v((4, 2, BLK, D), F32),
        v((2, 4, BLK, D), BF),
        v((ROWS, D), BF),
        v((2, POS, 2 * AW), BF),
        v((2, POS, AW), BF),
        v((4, BLK, AW), BF),
        v((2, POS, AW), BF),
        v((2, 4, BLK, AW), BF),
        v((ROWS, 128), F32),
        v((POS, 128), F32),
        v((ROWS, H), F32),
        v((NCH, H, CH), F32),
        v((NCH, H, CH), F32),
        v((N, D), F32),
        v((NCH, N, D), BF),
        v((N, D), BF),
        v((64, D), BF),
        v((64, D), BF),
        v((4, 16, D), BF),
        v((4, 16, D), F32),
        v((16, D), BF),
        v((4, 16, D), BF),
        v((4, 16, D), BF),
        v((4, 16, D), BF),
        v((64, D), BF),
        v((N, D), BF),
        v((8, 128), F32),
        v((8, 128), F32),
        v((8, 128), F32),
        v((4, 8, 128), F32),
        v((8, 128), F32),
        v((4, 8, 128), F32),
        dma((13,)),
        dma((2,)),
        dma((2, 4)),
        dma((2, 4)),
        dma((4,)),
        dma((4,)),
        dma((2, 4)),
        dma((2, 4)),
        dma((2,)),
        dma((2,)),
        dma((2, 4)),
        dma((2, 4)),
        dma((2, 4)),
        dma((2, 4)),
        dma((4,)),
        dma((4,)),
        dma,
        dma,
    ]
    out = pl.pallas_call(
        kernel,
        out_shape=jax.ShapeDtypeStruct((ROWS, D), BF),
        in_specs=[any_spec, any_spec, any_spec, vmem_spec, vmem_spec, any_spec, any_spec],
        out_specs=any_spec,
        scratch_shapes=scratch,
        compiler_params=pltpu.CompilerParams(
            collective_id=0, has_side_effects=True, vmem_limit_bytes=60 * 2**20
        ),
        cost_estimate=pl.CostEstimate(
            flops=12_000_000_000, bytes_accessed=24_000_000, transcendentals=4_000_000
        ),
    )(
        latents.reshape(ROWS, D),
        mixer_weight,
        step_weight,
        step_bias.reshape(1, H),
        decay_rate.reshape(1, H),
        attend_weight,
        output_weight,
    )
    return out.reshape(FR, BLK, D)


def solution(mesh):
    in_specs = (P("tm", "space", None), P(), P(), P(), P(), P(), P())
    out_specs = P("tm", "space", None)
    return jax.shard_map(
        on_device, mesh=mesh, in_specs=in_specs, out_specs=out_specs, check_vma=False
    )
```

```python
import math

import jax
import jax.numpy as jnp
from jax import lax
from jax.experimental import pallas as pl
from jax.experimental.pallas import tpu as pltpu
from jax.sharding import PartitionSpec as P

MESH = pl.DeviceIdType.MESH
BF = jnp.bfloat16
F32 = jnp.float32
EXACT = lax.Precision.HIGHEST

D = 1536
H = 12
HP = 128
N = 128
AH = 6
AW = AH * HP
FR = 8
BLK = 64
ROWS = FR * BLK
POS = 256
CH = 128
NCH = ROWS // CH
TM = 32
MIX_T = 896
Q_T = 768
KV_T = 768
OUT_T = 768
ATT_T = 768


def per_head(cols):
    rows = cols.shape[0]
    return jnp.concatenate(
        [jnp.broadcast_to(cols[:, h : h + 1], (rows, HP)) for h in range(H)], axis=1
    )


def pair(cols, h):
    shape = (cols.shape[0], HP)
    return jnp.concatenate(
        [jnp.broadcast_to(cols[:, i : i + 1], shape) for i in (h, h + 1)], axis=1
    )


def widen(v, width):
    return jnp.concatenate([v] * (width // 128), axis=1)


def inv_rms(x, eps):
    x = x.astype(F32)
    mean = jnp.sum(x * x, axis=-1, keepdims=True) * (1.0 / x.shape[-1])
    return jnp.broadcast_to(lax.rsqrt(mean + eps), (x.shape[0], 128))


def pair_mean():
    row = lax.broadcasted_iota(jnp.int32, (256, 256), 0)
    col = lax.broadcasted_iota(jnp.int32, (256, 256), 1)
    same = lax.div(row, 128) == lax.div(col, 128)
    return jnp.where(same, 1.0 / HP, 0.0).astype(BF)


def head_scaled(v, eps, mean_of):
    parts = []
    for j in range(0, v.shape[1], 256):
        p = v[:, j : j + 256]
        mean = jnp.dot((p * p).astype(BF), mean_of, preferred_element_type=F32)
        parts.append(p * lax.rsqrt(mean + eps))
    return parts[0] if len(parts) == 1 else jnp.concatenate(parts, axis=1)


def kernel(
    lat, wm_h, ws_h, bias_ref, rate_ref, wa_h, wo_h, out_h,
    xv, xt, wm, ws, wa, wo, u, yv, acc, ob, ssm,
    kv, qt, qe, at_send, at_recv,
    r_ref, rt_ref, la_ref, off_ref, lat_t, dt_t,
    s_ref, s_k, l_bf, a_recv, t_bf, b_recv, dec_ref, d_send, d_recv, e_send, s_in,
    ld_own, ld_a, ld_t, ld_b,
    load_sem, own_sem, x_ssem, x_rsem, q_ssem, q_rsem, at_ssem, at_rsem,
    a_ssem, a_rsem, b_ssem, b_rsem, d_ssem, d_rsem, e_ssem, e_rsem, answer_sem, go_sem,
):
    t = lax.axis_index("tm")
    y = lax.axis_index("space")
    core = lax.rem(t, 2)
    x = lax.rem(lax.div(t, 2), 4)
    z = lax.div(t, 8)
    t_next = lax.rem(t + 1, TM)
    t_prev = lax.rem(t + TM - 1, TM)
    ys = [lax.rem(y + d, 4) for d in range(4)]
    mate = (t + 1 - 2 * core, y)
    chip = z * 4 + x
    xs = [lax.rem(x + d, 4) for d in range(4)]
    zs = [lax.rem(z + d, 4) for d in range(4)]
    plane = [(i, j) for i in range(4) for j in range(4) if i + j > 0]

    def chip_dev(i, j):
        return (zs[i] * 8 + xs[j] * 2 + core, y)
    last = y == 3

    def remote(src, dst, ssem, rsem, dev):
        return pltpu.make_async_remote_copy(
            src_ref=src, dst_ref=dst, send_sem=ssem, recv_sem=rsem,
            device_id=dev, device_id_type=MESH,
        )

    loads = [
        pltpu.make_async_copy(src, dst, load_sem.at[i])
        for i, (src, dst) in enumerate([(lat, xv), (ws_h, ws), (wm_h, wm), (wa_h, wa), (wo_h, wo)])
    ]
    for i in (0, 1, 2):
        loads[i].start()

    mean_of = pair_mean()
    barrier = pltpu.get_barrier_semaphore()

    def greet(dev):
        pl.semaphore_signal(barrier, inc=1, device_id=dev, device_id_type=MESH)

    gateway = y == 0
    for d in (1, 2, 3):
        greet((t, ys[d]))

    @pl.when(gateway)
    def _():
        pl.semaphore_wait(answer_sem, 3)
        for i, j in plane:
            greet(chip_dev(i, j))
        greet((t_prev, y))
        greet((t_next, y))

    @pl.when(jnp.logical_not(gateway))
    def _():
        pl.semaphore_wait(barrier, 3)
        pl.semaphore_signal(answer_sem, inc=1, device_id=(t, 0), device_id_type=MESH)

    def x_copy(i, d):
        return remote(
            lat.at[pl.ds(pl.multiple_of(128 * ys[d] + 64 * i, 64), 64), :],
            xt.at[i, pl.ds(pl.multiple_of(64 * y, 64), 64), :],
            x_ssem.at[i, d], x_rsem.at[i, d], (t, ys[d]),
        )

    def x_own(i):
        return pltpu.make_async_copy(
            lat.at[pl.ds(pl.multiple_of(128 * y + 64 * i, 64), 64), :],
            xt.at[i, pl.ds(pl.multiple_of(64 * y, 64), 64), :],
            own_sem.at[i],
        )

    for d in (2, 1, 3):
        x_copy(0, d).start()
    for d in (2, 1, 3):
        x_copy(1, d).start()
    x_own(0).start()
    x_own(1).start()
    loads[3].start()
    loads[4].start()

    loads[0].wait()

    def norm_rows(j, _):
        rs = pl.ds(pl.multiple_of(j * 64, 64), 64)
        r_ref[rs, :] = inv_rms(xv[rs, :], 1e-6)
        return 0

    lax.fori_loop(0, ROWS // 64, norm_rows, 0)
    loads[1].wait()
    loads[2].wait()

    steps = lax.dot_general(
        xv[...], ws[...], (((1,), (1,)), ((), ())), preferred_element_type=F32
    )
    steps = steps * r_ref[:, :H] + bias_ref[...]
    dt = jnp.maximum(steps, 0.0) + jnp.log(1.0 + jnp.exp(-jnp.abs(steps)))
    rate = rate_ref[...]
    row_id = lax.broadcasted_iota(jnp.int32, (CH, CH), 0)
    col_id = lax.broadcasted_iota(jnp.int32, (CH, CH), 1)
    causal = row_id >= col_id
    tri = jnp.where(causal, 1.0, 0.0).astype(F32)
    eye = jnp.where(row_id == col_id, 1.0, 0.0).astype(F32)
    offs = [jnp.zeros((1, H), F32)]
    ends = []
    fe = []
    for k in range(NCH):
        dt_k = dt[k * CH : (k + 1) * CH, :]
        a_k = -rate * dt_k
        la_k = jnp.dot(tri, a_k, precision=EXACT, preferred_element_type=F32)
        la_ref[k * CH : (k + 1) * CH, :] = la_k
        lat_t[k] = lax.dot_general(
            a_k, tri, (((0,), (1,)), ((), ())), precision=EXACT, preferred_element_type=F32
        )
        dt_t[k] = lax.dot_general(
            dt_k, eye, (((0,), (1,)), ((), ())), precision=EXACT, preferred_element_type=F32
        )
        end_k = la_k[CH - 1 : CH, :]
        ends.append(end_k)
        off_ref[k, 0:1, 0:H] = offs[-1]
        offs.append(offs[-1] + end_k)
        fe.append(jnp.exp(end_k - la_k) * dt_k)
    ld_own[...] = jnp.zeros((8, 128), F32)
    ld_t[...] = jnp.zeros((8, 128), F32)
    ld_own[0:1, 0:H] = offs[NCH]

    def mix(j, _):
        cs = pl.ds(pl.multiple_of(j * MIX_T, MIX_T), MIX_T)
        part = jnp.dot(xv[...], wm[:, cs], preferred_element_type=F32)
        u[:, cs] = (part * widen(r_ref[...], MIX_T)).astype(BF)
        return 0

    lax.fori_loop(0, (D + 2 * N) // MIX_T, mix, 0)

    @pl.when(gateway)
    def _():
        pl.semaphore_wait(barrier, 20)
        for d in (1, 2, 3):
            pl.semaphore_signal(go_sem, inc=1, device_id=(t, ys[d]), device_id_type=MESH)

    for k in range(NCH):
        rs = pl.ds(k * CH, CH)
        scaled = (per_head(fe[k]) * u[rs, :D].astype(F32)).astype(BF)
        add = lax.dot_general(
            u[rs, D : D + N], scaled, (((0,), (0,)), ((), ())), preferred_element_type=F32
        )
        if k == 0:
            s_k[0] = jnp.zeros((N, D), BF)
            s_ref[...] = add
        else:
            s_k[k] = s_ref[...].astype(BF)
            s_ref[...] = s_ref[...] * per_head(jnp.exp(ends[k])) + add
    l_bf[...] = s_ref[...].astype(BF)

    loads[3].wait()

    def q_even(j, _):
        cs = pl.ds(pl.multiple_of(j * Q_T, Q_T), Q_T)
        rows = xv[...].reshape(4, 2, BLK, D)[:, 0].reshape(4 * BLK, D)
        scale = r_ref[...].reshape(4, 2, BLK, 128)[:, 0].reshape(4 * BLK, 128)
        part = jnp.dot(rows, wa[:, cs], preferred_element_type=F32) * widen(scale, Q_T)
        qe[:, :, cs] = head_scaled(part, 1e-6, mean_of).astype(BF).reshape(4, BLK, Q_T)
        return 0

    def q_copy(k):
        dev = (t_prev, 3) if k == 0 else (t, k - 1)
        return remote(
            qe.at[k], qt.at[1, pl.ds(pl.multiple_of(64 * y, 64), 64), :],
            q_ssem.at[k], q_rsem.at[y], dev,
        )

    def q_own(k):
        return pltpu.make_async_copy(
            qe.at[k], qt.at[1, pl.ds(pl.multiple_of(64 * y, 64), 64), :], q_rsem.at[y]
        )

    def diag(k, _):
        rs = pl.ds(pl.multiple_of(k * CH, CH), CH)
        cb = lax.dot_general(
            u[rs, D + N : D + 2 * N], u[rs, D : D + N], (((1,), (1,)), ((), ())),
            preferred_element_type=F32,
        )
        la_k = la_ref[rs, :]
        la_row = lat_t[k]
        dt_row = dt_t[k]
        for h in range(H):
            gap = la_k[:, h : h + 1] - la_row[h : h + 1, :]
            w = jnp.exp(jnp.where(causal, gap, -1e30)) * cb * dt_row[h : h + 1, :]
            yv[rs, h * HP : (h + 1) * HP] = jnp.dot(
                w.astype(BF), u[rs, h * HP : (h + 1) * HP], preferred_element_type=F32
            )
        return 0


    def attend_proj(i, width_from, dst, dst_from, tiles, scaled_tiles):
        def body(j, _):
            src = pl.ds(pl.multiple_of(width_from + j * KV_T, KV_T), KV_T)
            to = pl.ds(pl.multiple_of(dst_from + j * KV_T, KV_T), KV_T)
            part = jnp.dot(xt[i], wa[:, src], preferred_element_type=F32)
            part = part * widen(rt_ref[...], KV_T)
            if scaled_tiles:
                part = head_scaled(part, 1e-6, mean_of)
            dst[i, :, to] = part.astype(BF)
            return 0

        lax.fori_loop(0, tiles, body, 0)

    def norm_frame(i):
        def body(j, _):
            rs = pl.ds(pl.multiple_of(j * 64, 64), 64)
            rt_ref[rs, :] = inv_rms(xt[i, rs, :], 1e-6)
            return 0

        lax.fori_loop(0, POS // 64, body, 0)

    def frame_arrived(i):
        for d in (1, 2, 3):
            x_copy(i, d).wait_recv()
        x_own(i).wait()

    half = pl.ds(pl.multiple_of(64 * core, 64), 64)
    other_half = pl.ds(pl.multiple_of(64 - 64 * core, 64), 64)
    a_copy = remote(l_bf.at[other_half, :], a_recv, a_ssem.at[0], a_rsem.at[0], mate)
    ld_copy = remote(ld_own, ld_a, a_ssem.at[1], a_rsem.at[1], mate)

    @pl.when(jnp.logical_not(gateway))
    def _():
        pl.semaphore_wait(go_sem, 1)

    ld_copy.start()
    a_copy.start()

    for d in (1, 2, 3):
        x_copy(0, d).wait_send()


    lax.fori_loop(0, 2, diag, 0)

    a_copy.wait()
    ld_copy.wait()
    first = core == 0
    ld_mine = ld_own[0:1, 0:H]
    ld_theirs = ld_a[0:1, 0:H]
    ld0 = jnp.where(first, ld_mine, ld_theirs)
    ld1 = jnp.where(first, ld_theirs, ld_mine)
    ld_t[0:1, 0:H] = ld0 + ld1
    ld_b[chip] = ld_t[...]
    ld_copies = [remote(ld_t, ld_b.at[chip], b_ssem.at[1], b_rsem.at[1], chip_dev(i, j)) for i, j in plane]
    for cp in ld_copies:
        cp.start()

    mine = s_ref[half, :]
    theirs = a_recv[...].astype(F32)
    l0 = jnp.where(first, mine, theirs)
    l1 = jnp.where(first, theirs, mine)
    t_bf[...] = (per_head(jnp.exp(ld1)) * l0 + l1).astype(BF)

    def piece(ref, i, j):
        rows = pl.ds(pl.multiple_of(16 * j, 16), 16)
        lanes = pl.ds(pl.multiple_of(384 * i, 128), 384)
        return ref.at[rows, lanes]

    b_recv[chip] = t_bf[pl.ds(pl.multiple_of(16 * x, 16), 16), pl.ds(pl.multiple_of(384 * z, 128), 384)]
    for i, j in plane:
        remote(piece(t_bf, zs[i], xs[j]), b_recv.at[chip], b_ssem.at[0], b_rsem.at[0], chip_dev(i, j)).start()

    lax.fori_loop(0, AW // Q_T, q_even, 0)

    q_copy(0).start()
    for k in (1, 2, 3):

        @pl.when(y != k - 1)
        def _(k=k):
            q_copy(k).start()

        @pl.when(y == k - 1)
        def _(k=k):
            q_own(k).start()

    lax.fori_loop(2, 4, diag, 0)
    frame_arrived(0)
    norm_frame(0)
    attend_proj(0, AW, kv, 0, AW // KV_T, True)

    attend_proj(0, 2 * AW, kv, AW, AW // KV_T, False)

    def all_arrived(buf, ssem, rsem):
        part = buf.at[pl.ds(0, 15)]
        pltpu.make_async_copy(part, part, ssem).wait()
        pltpu.make_async_copy(part, part, rsem).wait()

    all_arrived(ld_b, b_ssem.at[1], b_rsem.at[1])
    all_arrived(b_recv, b_ssem.at[0], b_rsem.at[0])
    dec_ref[...] = per_head(jnp.exp(ld_b[:, 0, 0:H]))
    own_lanes = pl.ds(pl.multiple_of(384 * z, 128), 384)
    run = jnp.zeros((16, 384), F32)
    for j in range(16):
        d_send[j] = run.astype(BF)
        run = run * dec_ref[j : j + 1, own_lanes] + b_recv[j].astype(F32)
    own_rows = pl.ds(pl.multiple_of(16 * x, 16), 16)
    d_recv[own_rows, own_lanes] = d_send[chip]
    for i, j in plane:
        remote(
            d_send.at[zs[i] * 4 + xs[j]], piece(d_recv, z, x), d_ssem, d_rsem, chip_dev(i, j)
        ).start()

    frame_arrived(1)
    for d in (1, 2, 3):
        x_copy(1, d).wait_send()
    norm_frame(1)


    def q_odd(j, _):
        cs = pl.ds(pl.multiple_of(j * Q_T, Q_T), Q_T)
        part = jnp.dot(xt[1], wa[:, cs], preferred_element_type=F32) * widen(rt_ref[...], Q_T)
        qt[0, :, cs] = head_scaled(part, 1e-6, mean_of).astype(BF)
        return 0

    lax.fori_loop(0, AW // Q_T, q_odd, 0)

    def attention(i):
        for h in range(AH):
            hs = slice(h * HP, (h + 1) * HP)
            vs = slice(AW + h * HP, AW + (h + 1) * HP)
            s = lax.dot_general(
                qt[i, :, hs], kv[i, :, hs], (((1,), (1,)), ((), ())), preferred_element_type=F32
            )
            p = jnp.exp(s * (1.0 / math.sqrt(HP)))
            total = jnp.sum(p, axis=-1, keepdims=True)
            num = jnp.dot(p.astype(BF), kv[i, :, vs], preferred_element_type=F32)
            at_send[i, :, hs] = (num / total).astype(BF)

    def at_copy(i, d):
        src = at_send.at[i, pl.ds(pl.multiple_of(64 * ys[d], 64), 64), :]
        if i == 0:
            return remote(src, at_recv.at[1, y], at_ssem.at[i, d], at_rsem.at[1, y], (t, ys[d]))
        owner = jnp.where(last, t_next, t)
        k = ys[1]
        return remote(src, at_recv.at[0, k], at_ssem.at[i, d], at_rsem.at[0, k], (owner, ys[d]))

    def at_own(i):
        src = at_send.at[i, pl.ds(pl.multiple_of(64 * y, 64), 64), :]
        if i == 0:
            return pltpu.make_async_copy(src, at_recv.at[1, y], at_rsem.at[1, y])
        return pltpu.make_async_copy(src, at_recv.at[0, ys[1]], at_rsem.at[0, ys[1]])

    attention(0)
    for d in (2, 1, 3):
        at_copy(0, d).start()
    at_own(0).start()

    attend_proj(1, AW, kv, 0, AW // KV_T, True)
    attend_proj(1, 2 * AW, kv, AW, AW // KV_T, False)
    all_arrived(d_send, d_ssem, d_rsem)
    inc0 = d_recv[...].astype(F32)
    inc1 = per_head(jnp.exp(ld0)) * inc0 + l0
    e_send[...] = jnp.where(first, inc1, inc0).astype(BF)
    s_in[half, :] = jnp.where(first, inc0, inc1).astype(BF)
    e_copy = remote(e_send, s_in.at[half, :], e_ssem, e_rsem, mate)
    e_copy.start()

    for k in range(4):
        pltpu.make_async_copy(qe.at[k], qt.at[1, pl.ds(64 * k, 64), :], q_rsem.at[k]).wait()
    attention(1)
    for d in (2, 1, 3):
        at_copy(1, d).start()

    @pl.when(last)
    def _():
        at_copy(1, 0).start()

    @pl.when(jnp.logical_not(last))
    def _():
        at_own(1).start()

    e_copy.wait()


    def mixed(k, _):
        rs = pl.ds(pl.multiple_of(k * CH, CH), CH)
        c_k = u[rs, D + N : D + 2 * N]
        e_k = jnp.exp(la_ref[rs, :])
        e_in = jnp.exp(off_ref[k][0:1, 0:H])
        for h in range(0, H, 2):
            hs = slice(h * HP, (h + 2) * HP)
            state = s_k[k, :, hs].astype(F32) + pair(e_in, h) * s_in[:, hs].astype(F32)
            carried = jnp.dot(c_k, state.astype(BF), preferred_element_type=F32)
            m = yv[rs, hs] + pair(e_k, h) * carried
            ssm[rs, hs] = head_scaled(m, 1e-5, mean_of).astype(BF)
        return 0

    lax.fori_loop(0, NCH, mixed, 0)

    loads[4].wait()

    def out_ssm(j, _):
        cs = pl.ds(pl.multiple_of(j * OUT_T, OUT_T), OUT_T)
        part = jnp.dot(ssm[...], wo[:D, cs], preferred_element_type=F32)
        acc[:, :, :, cs] = (part + xv[:, cs].astype(F32)).reshape(4, 2, BLK, OUT_T)
        return 0

    lax.fori_loop(0, D // OUT_T, out_ssm, 0)

    out_copies = []
    for par in (1, 0):
        for k in range(4):
            pltpu.make_async_copy(at_send.at[0, pl.ds(0, 64), :], at_recv.at[par, k], at_rsem.at[par, k]).wait()
        if par == 0:

            @pl.when(t == 0)
            def _():
                at_recv[0, 0] = jnp.zeros((BLK, AW), BF)

        def out_att(j, _, par=par):
            cs = pl.ds(pl.multiple_of(j * ATT_T, ATT_T), ATT_T)
            rows = at_recv[par].reshape(4 * BLK, AW)
            part = jnp.dot(rows, wo[D:, cs], preferred_element_type=F32)
            ob[par, :, :, cs] = (part.reshape(4, BLK, ATT_T) + acc[:, par, :, cs]).astype(BF)
            return 0

        lax.fori_loop(0, D // ATT_T, out_att, 0)
        for k in range(4):
            cp = pltpu.make_async_copy(
                ob.at[par, k], out_h.at[pl.ds(128 * k + 64 * par, 64), :], load_sem.at[5 + 4 * par + k]
            )
            cp.start()
            out_copies.append(cp)

    for i in range(2):
        for d in (1, 2, 3):
            at_copy(i, d).wait_send()

    @pl.when(last)
    def _():
        at_copy(1, 0).wait_send()

    q_copy(0).wait_send()
    for k in (1, 2, 3):

        @pl.when(y != k - 1)
        def _(k=k):
            q_copy(k).wait_send()

    for cp in out_copies:
        cp.wait()


def on_device(latents, mixer_weight, step_weight, step_bias, decay_rate, attend_weight, output_weight):
    any_spec = pl.BlockSpec(memory_space=pl.ANY)
    vmem_spec = pl.BlockSpec(memory_space=pltpu.VMEM)
    dma = pltpu.SemaphoreType.DMA
    v = pltpu.VMEM
    scratch = [
        v((ROWS, D), BF),
        v((2, POS, D), BF),
        v((D, D + 2 * N), BF),
        v((H, D), BF),
        v((D, 3 * AW), BF),
        v((D + AW, D), BF),
        v((ROWS, D + 2 * N), BF),
        v((ROWS, D), F32),
        v((4, 2, BLK, D), F32),
        v((2, 4, BLK, D), BF),
        v((ROWS, D), BF),
        v((2, POS, 2 * AW), BF),
        v((2, POS, AW), BF),
        v((4, BLK, AW), BF),
        v((2, POS, AW), BF),
        v((2, 4, BLK, AW), BF),
        v((ROWS, 128), F32),
        v((POS, 128), F32),
        v((ROWS, H), F32),
        v((NCH, 8, 128), F32),
        v((NCH, H, CH), F32),
        v((NCH, H, CH), F32),
        v((N, D), F32),
        v((NCH, N, D), BF),
        v((N, D), BF),
        v((64, D), BF),
        v((64, D), BF),
        v((16, 16, 384), BF),
        v((16, D), F32),
        v((16, 16, 384), BF),
        v((64, D), BF),
        v((64, D), BF),
        v((N, D), BF),
        v((8, 128), F32),
        v((8, 128), F32),
        v((8, 128), F32),
        v((16, 8, 128), F32),
        dma((13,)),
        dma((2,)),
        dma((2, 4)),
        dma((2, 4)),
        dma((4,)),
        dma((4,)),
        dma((2, 4)),
        dma((2, 4)),
        dma((2,)),
        dma((2,)),
        dma((2,)),
        dma((2,)),
        dma,
        dma,
        dma,
        dma,
        pltpu.SemaphoreType.REGULAR,
        pltpu.SemaphoreType.REGULAR,
    ]
    out = pl.pallas_call(
        kernel,
        out_shape=jax.ShapeDtypeStruct((ROWS, D), BF),
        in_specs=[any_spec, any_spec, any_spec, vmem_spec, vmem_spec, any_spec, any_spec],
        out_specs=any_spec,
        scratch_shapes=scratch,
        compiler_params=pltpu.CompilerParams(
            collective_id=0, has_side_effects=True, vmem_limit_bytes=60 * 2**20
        ),
        cost_estimate=pl.CostEstimate(
            flops=12_000_000_000, bytes_accessed=24_000_000, transcendentals=4_000_000
        ),
    )(
        latents.reshape(ROWS, D),
        mixer_weight,
        step_weight.T,
        step_bias.reshape(1, H),
        decay_rate.reshape(1, H),
        attend_weight,
        output_weight,
    )
    return out.reshape(FR, BLK, D)


def solution(mesh):
    in_specs = (P("tm", "space", None), P(), P(), P(), P(), P(), P())
    out_specs = P("tm", "space", None)
    return jax.shard_map(
        on_device, mesh=mesh, in_specs=in_specs, out_specs=out_specs, check_vma=False
    )
```

```python
import math

import jax
import jax.numpy as jnp
from jax import lax
from jax.experimental import pallas as pl
from jax.experimental.pallas import tpu as pltpu
from jax.sharding import PartitionSpec as P

MESH = pl.DeviceIdType.MESH
BF = jnp.bfloat16
F32 = jnp.float32
EXACT = lax.Precision.HIGHEST

D = 1536
H = 12
HP = 128
N = 128
AH = 6
AW = AH * HP
FR = 8
BLK = 64
ROWS = FR * BLK
POS = 256
CH = 128
NCH = ROWS // CH
TM = 32
MIX_T = 896
Q_T = 768
KV_T = 768
OUT_T = 1536
ATT_T = 1536


def per_head(cols):
    rows = cols.shape[0]
    return jnp.concatenate(
        [jnp.broadcast_to(cols[:, h : h + 1], (rows, HP)) for h in range(H)], axis=1
    )


def pair(cols, h):
    shape = (cols.shape[0], HP)
    return jnp.concatenate(
        [jnp.broadcast_to(cols[:, i : i + 1], shape) for i in (h, h + 1)], axis=1
    )


def widen(v, width):
    return jnp.concatenate([v] * (width // 128), axis=1)


def inv_rms(x, eps):
    x = x.astype(F32)
    mean = jnp.sum(x * x, axis=-1, keepdims=True) * (1.0 / x.shape[-1])
    return jnp.broadcast_to(lax.rsqrt(mean + eps), (x.shape[0], 128))


def pair_mean():
    row = lax.broadcasted_iota(jnp.int32, (256, 256), 0)
    col = lax.broadcasted_iota(jnp.int32, (256, 256), 1)
    same = lax.div(row, 128) == lax.div(col, 128)
    return jnp.where(same, 1.0 / HP, 0.0).astype(BF)


def head_scaled(v, eps, mean_of):
    parts = []
    for j in range(0, v.shape[1], 256):
        p = v[:, j : j + 256]
        mean = jnp.dot((p * p).astype(BF), mean_of, preferred_element_type=F32)
        parts.append(p * lax.rsqrt(mean + eps))
    return parts[0] if len(parts) == 1 else jnp.concatenate(parts, axis=1)


def kernel(
    lat, wm_h, ws_h, bias_ref, rate_ref, wa_h, wo_h, out_ref,
    xv, xt, wm, ws, wa, wo, u, yv, acc, ssm,
    kv, qt, qe, at_send, at_recv,
    r_ref, rt_ref, la_ref, off_ref, lat_t, dt_t,
    s_ref, s_k, l_bf, a_recv, t_bf, b_recv, dec_ref, d_send, d_recv, e_send, s_in,
    ld_own, ld_a, ld_t, ld_b,
    load_sem, own_sem, x_ssem, x_rsem, q_ssem, q_rsem, at_ssem, at_rsem,
    a_ssem, a_rsem, b_ssem, b_rsem, d_ssem, d_rsem, e_ssem, e_rsem, answer_sem, go_sem,
):
    t = lax.axis_index("tm")
    y = lax.axis_index("space")
    core = lax.rem(t, 2)
    x = lax.rem(lax.div(t, 2), 4)
    z = lax.div(t, 8)
    t_next = lax.rem(t + 1, TM)
    t_prev = lax.rem(t + TM - 1, TM)
    ys = [lax.rem(y + d, 4) for d in range(4)]
    mate = (t + 1 - 2 * core, y)
    chip = z * 4 + x
    xs = [lax.rem(x + d, 4) for d in range(4)]
    zs = [lax.rem(z + d, 4) for d in range(4)]
    plane = [(i, j) for i in range(4) for j in range(4) if i + j > 0]

    def chip_dev(i, j):
        return (zs[i] * 8 + xs[j] * 2 + core, y)
    last = y == 3
    followed = jnp.logical_or(t < TM - 1, y < 3)

    def remote(src, dst, ssem, rsem, dev):
        return pltpu.make_async_remote_copy(
            src_ref=src, dst_ref=dst, send_sem=ssem, recv_sem=rsem,
            device_id=dev, device_id_type=MESH,
        )

    loads = [
        pltpu.make_async_copy(src, dst, load_sem.at[i])
        for i, (src, dst) in enumerate([(lat, xv), (ws_h, ws), (wm_h, wm), (wa_h, wa), (wo_h, wo)])
    ]
    for i in (0, 1, 2):
        loads[i].start()

    mean_of = pair_mean()
    barrier = pltpu.get_barrier_semaphore()

    def greet(dev):
        pl.semaphore_signal(barrier, inc=1, device_id=dev, device_id_type=MESH)

    gateway = y == 0
    for d in (1, 2, 3):
        greet((t, ys[d]))

    @pl.when(gateway)
    def _():
        pl.semaphore_wait(answer_sem, 3)
        for i, j in plane:
            greet(chip_dev(i, j))
        greet((t_prev, y))
        greet((t_next, y))

    @pl.when(jnp.logical_not(gateway))
    def _():
        pl.semaphore_wait(barrier, 3)
        pl.semaphore_signal(answer_sem, inc=1, device_id=(t, 0), device_id_type=MESH)

    def x_copy(i, d):
        return remote(
            lat.at[pl.ds(pl.multiple_of(128 * ys[d] + 64 * i, 64), 64), :],
            xt.at[i, pl.ds(pl.multiple_of(64 * y, 64), 64), :],
            x_ssem.at[i, d], x_rsem.at[i, d], (t, ys[d]),
        )

    def x_own(i):
        return pltpu.make_async_copy(
            lat.at[pl.ds(pl.multiple_of(128 * y + 64 * i, 64), 64), :],
            xt.at[i, pl.ds(pl.multiple_of(64 * y, 64), 64), :],
            own_sem.at[i],
        )

    for d in (2, 1, 3):
        x_copy(0, d).start()
    for d in (2, 1, 3):
        x_copy(1, d).start()
    x_own(0).start()
    x_own(1).start()
    loads[3].start()
    loads[4].start()

    loads[0].wait()

    def norm_rows(j, _):
        rs = pl.ds(pl.multiple_of(j * 64, 64), 64)
        r_ref[rs, :] = inv_rms(xv[rs, :], 1e-6)
        return 0

    lax.fori_loop(0, ROWS // 64, norm_rows, 0)
    loads[1].wait()
    loads[2].wait()

    steps = lax.dot_general(
        xv[...], ws[...], (((1,), (1,)), ((), ())), preferred_element_type=F32
    )
    steps = steps * r_ref[:, :H] + bias_ref[...]
    dt = jnp.maximum(steps, 0.0) + jnp.log(1.0 + jnp.exp(-jnp.abs(steps)))
    rate = rate_ref[...]
    row_id = lax.broadcasted_iota(jnp.int32, (CH, CH), 0)
    col_id = lax.broadcasted_iota(jnp.int32, (CH, CH), 1)
    causal = row_id >= col_id
    tri = jnp.where(causal, 1.0, 0.0).astype(F32)
    eye = jnp.where(row_id == col_id, 1.0, 0.0).astype(F32)
    offs = [jnp.zeros((1, H), F32)]
    ends = []
    fe = []
    for k in range(NCH):
        dt_k = dt[k * CH : (k + 1) * CH, :]
        a_k = -rate * dt_k
        la_k = jnp.dot(tri, a_k, precision=EXACT, preferred_element_type=F32)
        la_ref[k * CH : (k + 1) * CH, :] = la_k
        end_k = la_k[CH - 1 : CH, :]
        ends.append(end_k)
        off_ref[k, 0:1, 0:H] = offs[-1]
        offs.append(offs[-1] + end_k)
        fe.append(jnp.exp(end_k - la_k) * dt_k)
    ld_own[...] = jnp.zeros((8, 128), F32)
    ld_t[...] = jnp.zeros((8, 128), F32)
    ld_own[0:1, 0:H] = offs[NCH]

    def mix(j, _):
        cs = pl.ds(pl.multiple_of(j * MIX_T, MIX_T), MIX_T)
        part = jnp.dot(xv[...], wm[:, cs], preferred_element_type=F32)
        u[:, cs] = (part * widen(r_ref[...], MIX_T)).astype(BF)
        return 0

    lax.fori_loop(0, (D + 2 * N) // MIX_T, mix, 0)

    @pl.when(gateway)
    def _():
        pl.semaphore_wait(barrier, 20)
        for d in (1, 2, 3):
            pl.semaphore_signal(go_sem, inc=1, device_id=(t, ys[d]), device_id_type=MESH)

    for k in range(NCH):
        rs = pl.ds(k * CH, CH)
        scaled = (per_head(fe[k]) * u[rs, :D].astype(F32)).astype(BF)
        add = lax.dot_general(
            u[rs, D : D + N], scaled, (((0,), (0,)), ((), ())), preferred_element_type=F32
        )
        if k == 0:
            s_k[0] = jnp.zeros((N, D), BF)
            s_ref[...] = add
        else:
            s_k[k] = s_ref[...].astype(BF)
            s_ref[...] = s_ref[...] * per_head(jnp.exp(ends[k])) + add
    l_bf[...] = s_ref[...].astype(BF)

    loads[3].wait()

    def q_even(j, _):
        cs = pl.ds(pl.multiple_of(j * Q_T, Q_T), Q_T)
        rows = xv[...].reshape(4, 2, BLK, D)[:, 0].reshape(4 * BLK, D)
        scale = r_ref[...].reshape(4, 2, BLK, 128)[:, 0].reshape(4 * BLK, 128)
        part = jnp.dot(rows, wa[:, cs], preferred_element_type=F32) * widen(scale, Q_T)
        qe[:, :, cs] = head_scaled(part, 1e-6, mean_of).astype(BF).reshape(4, BLK, Q_T)
        return 0

    def q_copy(k):
        dev = (t_prev, 3) if k == 0 else (t, k - 1)
        return remote(
            qe.at[k], qt.at[1, pl.ds(pl.multiple_of(64 * y, 64), 64), :],
            q_ssem.at[k], q_rsem.at[y], dev,
        )

    def q_own(k):
        return pltpu.make_async_copy(
            qe.at[k], qt.at[1, pl.ds(pl.multiple_of(64 * y, 64), 64), :], q_rsem.at[y]
        )

    def diag(k, _):
        rs = pl.ds(pl.multiple_of(k * CH, CH), CH)
        cb = lax.dot_general(
            u[rs, D + N : D + 2 * N], u[rs, D : D + N], (((1,), (1,)), ((), ())),
            preferred_element_type=F32,
        )
        la_k = la_ref[rs, :]
        la_row = lat_t[k]
        dt_row = dt_t[k]
        for h in range(H):
            gap = la_k[:, h : h + 1] - la_row[h : h + 1, :]
            w = jnp.exp(jnp.where(causal, gap, -1e30)) * cb * dt_row[h : h + 1, :]
            yv[rs, h * HP : (h + 1) * HP] = jnp.dot(
                w.astype(BF), u[rs, h * HP : (h + 1) * HP], preferred_element_type=F32
            )
        return 0


    def attend_proj(i, width_from, dst, dst_from, tiles, scaled_tiles):
        def body(j, _):
            src = pl.ds(pl.multiple_of(width_from + j * KV_T, KV_T), KV_T)
            to = pl.ds(pl.multiple_of(dst_from + j * KV_T, KV_T), KV_T)
            part = jnp.dot(xt[i], wa[:, src], preferred_element_type=F32)
            part = part * widen(rt_ref[...], KV_T)
            if scaled_tiles:
                part = head_scaled(part, 1e-6, mean_of)
            dst[i, :, to] = part.astype(BF)
            return 0

        lax.fori_loop(0, tiles, body, 0)

    def norm_frame(i):
        def body(j, _):
            rs = pl.ds(pl.multiple_of(j * 64, 64), 64)
            rt_ref[rs, :] = inv_rms(xt[i, rs, :], 1e-6)
            return 0

        lax.fori_loop(0, POS // 64, body, 0)

    def frame_arrived(i):
        for d in (1, 2, 3):
            x_copy(i, d).wait_recv()
        x_own(i).wait()

    half = pl.ds(pl.multiple_of(64 * core, 64), 64)
    other_half = pl.ds(pl.multiple_of(64 - 64 * core, 64), 64)
    a_copy = remote(l_bf.at[other_half, :], a_recv, a_ssem.at[0], a_rsem.at[0], mate)
    ld_copy = remote(ld_own, ld_a, a_ssem.at[1], a_rsem.at[1], mate)

    @pl.when(jnp.logical_not(gateway))
    def _():
        pl.semaphore_wait(go_sem, 1)

    ld_copy.start()
    a_copy.start()

    for k in range(NCH):
        dt_k = dt[k * CH : (k + 1) * CH, :]
        a_k = -rate * dt_k
        lat_t[k] = lax.dot_general(
            a_k, tri, (((0,), (1,)), ((), ())), precision=EXACT, preferred_element_type=F32
        )
        dt_t[k] = lax.dot_general(
            dt_k, eye, (((0,), (1,)), ((), ())), precision=EXACT, preferred_element_type=F32
        )


    a_copy.wait()
    ld_copy.wait()
    first = core == 0
    ld_mine = ld_own[0:1, 0:H]
    ld_theirs = ld_a[0:1, 0:H]
    ld0 = jnp.where(first, ld_mine, ld_theirs)
    ld1 = jnp.where(first, ld_theirs, ld_mine)
    ld_t[0:1, 0:H] = ld0 + ld1
    ld_b[chip] = ld_t[...]
    ld_copies = [remote(ld_t, ld_b.at[chip], b_ssem.at[1], b_rsem.at[1], chip_dev(i, j)) for i, j in plane]
    for cp in ld_copies:
        cp.start()

    mine = s_ref[half, :]
    theirs = a_recv[...].astype(F32)
    l0 = jnp.where(first, mine, theirs)
    l1 = jnp.where(first, theirs, mine)
    t_bf[...] = (per_head(jnp.exp(ld1)) * l0 + l1).astype(BF)

    def piece(ref, i, j):
        rows = pl.ds(pl.multiple_of(16 * j, 16), 16)
        lanes = pl.ds(pl.multiple_of(384 * i, 128), 384)
        return ref.at[rows, lanes]

    b_recv[chip] = t_bf[pl.ds(pl.multiple_of(16 * x, 16), 16), pl.ds(pl.multiple_of(384 * z, 128), 384)]
    for i, j in plane:
        remote(piece(t_bf, zs[i], xs[j]), b_recv.at[chip], b_ssem.at[0], b_rsem.at[0], chip_dev(i, j)).start()

    lax.fori_loop(0, AW // Q_T, q_even, 0)

    @pl.when(t > 0)
    def _():
        q_copy(0).start()

    for k in (1, 2, 3):

        @pl.when(y != k - 1)
        def _(k=k):
            q_copy(k).start()

        @pl.when(y == k - 1)
        def _(k=k):
            q_own(k).start()

    lax.fori_loop(0, 4, diag, 0)
    frame_arrived(0)
    norm_frame(0)
    attend_proj(0, AW, kv, 0, AW // KV_T, True)

    attend_proj(0, 2 * AW, kv, AW, AW // KV_T, False)

    def all_arrived(buf, ssem, rsem):
        part = buf.at[pl.ds(0, 15)]
        pltpu.make_async_copy(part, part, ssem).wait()
        pltpu.make_async_copy(part, part, rsem).wait()

    all_arrived(ld_b, b_ssem.at[1], b_rsem.at[1])
    all_arrived(b_recv, b_ssem.at[0], b_rsem.at[0])
    dec_ref[...] = per_head(jnp.exp(ld_b[:, 0, 0:H]))
    own_lanes = pl.ds(pl.multiple_of(384 * z, 128), 384)
    run = jnp.zeros((16, 384), F32)
    for j in range(16):
        d_send[j] = run.astype(BF)
        run = run * dec_ref[j : j + 1, own_lanes] + b_recv[j].astype(F32)
    own_rows = pl.ds(pl.multiple_of(16 * x, 16), 16)
    d_recv[own_rows, own_lanes] = d_send[chip]
    for i, j in plane:
        remote(
            d_send.at[zs[i] * 4 + xs[j]], piece(d_recv, z, x), d_ssem, d_rsem, chip_dev(i, j)
        ).start()

    frame_arrived(1)
    norm_frame(1)


    def q_odd(j, _):
        cs = pl.ds(pl.multiple_of(j * Q_T, Q_T), Q_T)
        part = jnp.dot(xt[1], wa[:, cs], preferred_element_type=F32) * widen(rt_ref[...], Q_T)
        qt[0, :, cs] = head_scaled(part, 1e-6, mean_of).astype(BF)
        return 0

    lax.fori_loop(0, AW // Q_T, q_odd, 0)

    def attention(i):
        for h in range(AH):
            hs = slice(h * HP, (h + 1) * HP)
            vs = slice(AW + h * HP, AW + (h + 1) * HP)
            s = lax.dot_general(
                qt[i, :, hs], kv[i, :, hs], (((1,), (1,)), ((), ())), preferred_element_type=F32
            )
            p = jnp.exp(s * (1.0 / math.sqrt(HP)))
            total = jnp.sum(p, axis=-1, keepdims=True)
            num = jnp.dot(p.astype(BF), kv[i, :, vs], preferred_element_type=F32)
            at_send[i, :, hs] = (num / total).astype(BF)

    def at_copy(i, d):
        src = at_send.at[i, pl.ds(pl.multiple_of(64 * ys[d], 64), 64), :]
        if i == 0:
            return remote(src, at_recv.at[1, y], at_ssem.at[i, d], at_rsem.at[1, y], (t, ys[d]))
        owner = jnp.where(last, t_next, t)
        k = ys[1]
        return remote(src, at_recv.at[0, k], at_ssem.at[i, d], at_rsem.at[0, k], (owner, ys[d]))

    def at_own(i):
        src = at_send.at[i, pl.ds(pl.multiple_of(64 * y, 64), 64), :]
        if i == 0:
            return pltpu.make_async_copy(src, at_recv.at[1, y], at_rsem.at[1, y])
        return pltpu.make_async_copy(src, at_recv.at[0, ys[1]], at_rsem.at[0, ys[1]])

    attention(0)
    for d in (2, 1, 3):
        at_copy(0, d).start()
    at_own(0).start()

    attend_proj(1, AW, kv, 0, AW // KV_T, True)
    attend_proj(1, 2 * AW, kv, AW, AW // KV_T, False)
    all_arrived(d_send, d_ssem, d_rsem)
    inc0 = d_recv[...].astype(F32)
    inc1 = per_head(jnp.exp(ld0)) * inc0 + l0
    e_send[...] = jnp.where(first, inc1, inc0).astype(BF)
    s_in[half, :] = jnp.where(first, inc0, inc1).astype(BF)
    e_copy = remote(e_send, s_in.at[half, :], e_ssem, e_rsem, mate)
    e_copy.start()

    @pl.when(followed)
    def _():
        for k in range(4):
            pltpu.make_async_copy(qe.at[k], qt.at[1, pl.ds(64 * k, 64), :], q_rsem.at[k]).wait()
        attention(1)
        for d in (2, 1, 3):
            at_copy(1, d).start()

    @pl.when(jnp.logical_and(last, followed))
    def _():
        at_copy(1, 0).start()

    @pl.when(jnp.logical_not(last))
    def _():
        at_own(1).start()

    e_copy.wait()


    def mixed(k, _):
        rs = pl.ds(pl.multiple_of(k * CH, CH), CH)
        c_k = u[rs, D + N : D + 2 * N]
        e_k = jnp.exp(la_ref[rs, :])
        e_in = jnp.exp(off_ref[k][0:1, 0:H])
        for h in range(0, H, 2):
            hs = slice(h * HP, (h + 2) * HP)
            state = s_k[k, :, hs].astype(F32) + pair(e_in, h) * s_in[:, hs].astype(F32)
            carried = jnp.dot(c_k, state.astype(BF), preferred_element_type=F32)
            m = yv[rs, hs] + pair(e_k, h) * carried
            ssm[rs, hs] = head_scaled(m, 1e-5, mean_of).astype(BF)
        return 0

    lax.fori_loop(0, NCH, mixed, 0)

    loads[4].wait()

    def out_ssm(j, _):
        cs = pl.ds(pl.multiple_of(j * OUT_T, OUT_T), OUT_T)
        part = jnp.dot(ssm[...], wo[:D, cs], preferred_element_type=F32)
        acc[:, :, :, cs] = (part + xv[:, cs].astype(F32)).reshape(4, 2, BLK, OUT_T)
        return 0

    lax.fori_loop(0, D // OUT_T, out_ssm, 0)

    for par in (1, 0):
        for k in range(4):
            arrival = pltpu.make_async_copy(
                at_send.at[0, pl.ds(0, 64), :], at_recv.at[par, k], at_rsem.at[par, k]
            )
            if par == 1 or k > 0:
                arrival.wait()
                continue

            @pl.when(t > 0)
            def _(arrival=arrival):
                arrival.wait()

            @pl.when(t == 0)
            def _():
                at_recv[0, 0] = jnp.zeros((BLK, AW), BF)

        def out_att(j, _, par=par):
            cs = pl.ds(pl.multiple_of(j * ATT_T, ATT_T), ATT_T)
            rows = at_recv[par].reshape(4 * BLK, AW)
            part = jnp.dot(rows, wo[D:, cs], preferred_element_type=F32)
            out_ref[:, par, :, cs] = (part.reshape(4, BLK, ATT_T) + acc[:, par, :, cs]).astype(BF)
            return 0

        lax.fori_loop(0, D // ATT_T, out_att, 0)

    for i in range(2):
        for d in (1, 2, 3):
            x_copy(i, d).wait_send()
    for d in (1, 2, 3):
        at_copy(0, d).wait_send()

    @pl.when(followed)
    def _():
        for d in (1, 2, 3):
            at_copy(1, d).wait_send()

    @pl.when(jnp.logical_and(last, followed))
    def _():
        at_copy(1, 0).wait_send()

    @pl.when(t > 0)
    def _():
        q_copy(0).wait_send()

    for k in (1, 2, 3):

        @pl.when(y != k - 1)
        def _(k=k):
            q_copy(k).wait_send()


def on_device(latents, mixer_weight, step_weight, step_bias, decay_rate, attend_weight, output_weight):
    any_spec = pl.BlockSpec(memory_space=pl.ANY)
    vmem_spec = pl.BlockSpec(memory_space=pltpu.VMEM)
    dma = pltpu.SemaphoreType.DMA
    v = pltpu.VMEM
    scratch = [
        v((ROWS, D), BF),
        v((2, POS, D), BF),
        v((D, D + 2 * N), BF),
        v((H, D), BF),
        v((D, 3 * AW), BF),
        v((D + AW, D), BF),
        v((ROWS, D + 2 * N), BF),
        v((ROWS, D), F32),
        v((4, 2, BLK, D), F32),
        v((ROWS, D), BF),
        v((2, POS, 2 * AW), BF),
        v((2, POS, AW), BF),
        v((4, BLK, AW), BF),
        v((2, POS, AW), BF),
        v((2, 4, BLK, AW), BF),
        v((ROWS, 128), F32),
        v((POS, 128), F32),
        v((ROWS, H), F32),
        v((NCH, 8, 128), F32),
        v((NCH, H, CH), F32),
        v((NCH, H, CH), F32),
        v((N, D), F32),
        v((NCH, N, D), BF),
        v((N, D), BF),
        v((64, D), BF),
        v((64, D), BF),
        v((16, 16, 384), BF),
        v((16, D), F32),
        v((16, 16, 384), BF),
        v((64, D), BF),
        v((64, D), BF),
        v((N, D), BF),
        v((8, 128), F32),
        v((8, 128), F32),
        v((8, 128), F32),
        v((16, 8, 128), F32),
        dma((13,)),
        dma((2,)),
        dma((2, 4)),
        dma((2, 4)),
        dma((4,)),
        dma((4,)),
        dma((2, 4)),
        dma((2, 4)),
        dma((2,)),
        dma((2,)),
        dma((2,)),
        dma((2,)),
        dma,
        dma,
        dma,
        dma,
        pltpu.SemaphoreType.REGULAR,
        pltpu.SemaphoreType.REGULAR,
    ]
    out = pl.pallas_call(
        kernel,
        out_shape=pltpu.VMEM((4, 2, BLK, D), BF),
        in_specs=[any_spec, any_spec, any_spec, vmem_spec, vmem_spec, any_spec, any_spec],
        out_specs=vmem_spec,
        scratch_shapes=scratch,
        compiler_params=pltpu.CompilerParams(
            collective_id=0, has_side_effects=True, vmem_limit_bytes=60 * 2**20
        ),
        cost_estimate=pl.CostEstimate(
            flops=12_000_000_000, bytes_accessed=24_000_000, transcendentals=4_000_000
        ),
    )(
        latents.reshape(ROWS, D),
        mixer_weight,
        step_weight.T,
        step_bias.reshape(1, H),
        decay_rate.reshape(1, H),
        attend_weight,
        output_weight,
    )
    return out.reshape(FR, BLK, D)


def solution(mesh):
    in_specs = (P("tm", "space", None), P(), P(), P(), P(), P(), P())
    out_specs = P("tm", "space", None)
    return jax.shard_map(
        on_device, mesh=mesh, in_specs=in_specs, out_specs=out_specs, check_vma=False
    )
```

```python
import math

import jax
import jax.numpy as jnp
from jax import lax
from jax.experimental import pallas as pl
from jax.experimental.pallas import tpu as pltpu
from jax.sharding import PartitionSpec as P

MESH = pl.DeviceIdType.MESH
BF = jnp.bfloat16
F32 = jnp.float32
EXACT = lax.Precision.HIGHEST

D = 1536
H = 12
HP = 128
N = 128
AH = 6
AW = AH * HP
FR = 8
BLK = 64
ROWS = FR * BLK
POS = 256
CH = 128
NCH = ROWS // CH
TM = 32
MIX_T = 896
Q_T = 768
KV_T = 768
OUT_T = 1536
ATT_T = 1536


def per_head(cols):
    rows = cols.shape[0]
    return jnp.concatenate(
        [jnp.broadcast_to(cols[:, h : h + 1], (rows, HP)) for h in range(H)], axis=1
    )


def pair(cols, h):
    shape = (cols.shape[0], HP)
    return jnp.concatenate(
        [jnp.broadcast_to(cols[:, i : i + 1], shape) for i in (h, h + 1)], axis=1
    )


def widen(v, width):
    return jnp.concatenate([v] * (width // 128), axis=1)


def inv_rms(x, eps):
    x = x.astype(F32)
    mean = jnp.sum(x * x, axis=-1, keepdims=True) * (1.0 / x.shape[-1])
    return jnp.broadcast_to(lax.rsqrt(mean + eps), (x.shape[0], 128))


def pair_mean():
    row = lax.broadcasted_iota(jnp.int32, (256, 256), 0)
    col = lax.broadcasted_iota(jnp.int32, (256, 256), 1)
    same = lax.div(row, 128) == lax.div(col, 128)
    return jnp.where(same, 1.0 / HP, 0.0).astype(BF)


def head_scaled(v, eps, mean_of):
    parts = []
    for j in range(0, v.shape[1], 256):
        p = v[:, j : j + 256]
        mean = jnp.dot((p * p).astype(BF), mean_of, preferred_element_type=F32)
        parts.append(p * lax.rsqrt(mean + eps))
    return parts[0] if len(parts) == 1 else jnp.concatenate(parts, axis=1)


def kernel(
    lat, wm_h, ws_h, bias_ref, rate_ref, wa_h, wo_h, out_ref,
    xv, xt, wm, ws, wa, wo, u, yv, acc, ssm,
    kv, qt, qe, at_send, at_recv,
    r_ref, rt_ref, la_ref, off_ref, lat_t, dt_t,
    s_ref, s_k, l_bf, a_recv, t_bf, b_recv, dec_ref, d_send, d_recv, e_send, s_in,
    ld_own, ld_a, ld_t, ld_b,
    load_sem, own_sem, x_ssem, x_rsem, q_ssem, q_rsem, at_ssem, at_rsem,
    a_ssem, a_rsem, b_ssem, b_rsem, d_ssem, d_rsem, e_ssem, e_rsem, answer_sem, go_sem,
):
    t = lax.axis_index("tm")
    y = lax.axis_index("space")
    core = lax.rem(t, 2)
    x = lax.rem(lax.div(t, 2), 4)
    z = lax.div(t, 8)
    t_next = lax.rem(t + 1, TM)
    t_prev = lax.rem(t + TM - 1, TM)
    ys = [lax.rem(y + d, 4) for d in range(4)]
    mate = (t + 1 - 2 * core, y)
    chip = z * 4 + x
    xs = [lax.rem(x + d, 4) for d in range(4)]
    zs = [lax.rem(z + d, 4) for d in range(4)]
    plane = [(i, j) for i in range(4) for j in range(4) if i + j > 0]

    def chip_dev(i, j):
        return (zs[i] * 8 + xs[j] * 2 + core, y)
    last = y == 3
    followed = jnp.logical_or(t < TM - 1, y < 3)

    def remote(src, dst, ssem, rsem, dev):
        return pltpu.make_async_remote_copy(
            src_ref=src, dst_ref=dst, send_sem=ssem, recv_sem=rsem,
            device_id=dev, device_id_type=MESH,
        )

    loads = [
        pltpu.make_async_copy(src, dst, load_sem.at[i])
        for i, (src, dst) in enumerate([(lat, xv), (ws_h, ws), (wm_h, wm), (wa_h, wa), (wo_h, wo)])
    ]
    for i in (0, 1, 2):
        loads[i].start()

    mean_of = pair_mean()
    barrier = pltpu.get_barrier_semaphore()

    def greet(dev):
        pl.semaphore_signal(barrier, inc=1, device_id=dev, device_id_type=MESH)

    gateway = y == 0
    for d in (1, 2, 3):
        greet((t, ys[d]))

    @pl.when(gateway)
    def _():
        pl.semaphore_wait(answer_sem, 3)
        for i, j in plane:
            greet(chip_dev(i, j))
        greet((t_prev, y))
        greet((t_next, y))

    @pl.when(jnp.logical_not(gateway))
    def _():
        pl.semaphore_wait(barrier, 3)
        pl.semaphore_signal(answer_sem, inc=1, device_id=(t, 0), device_id_type=MESH)

    def x_copy(i, d):
        return remote(
            lat.at[pl.ds(pl.multiple_of(128 * ys[d] + 64 * i, 64), 64), :],
            xt.at[i, pl.ds(pl.multiple_of(64 * y, 64), 64), :],
            x_ssem.at[i, d], x_rsem.at[i, d], (t, ys[d]),
        )

    def x_own(i):
        return pltpu.make_async_copy(
            lat.at[pl.ds(pl.multiple_of(128 * y + 64 * i, 64), 64), :],
            xt.at[i, pl.ds(pl.multiple_of(64 * y, 64), 64), :],
            own_sem.at[i],
        )

    for d in (2, 1, 3):
        x_copy(0, d).start()
    for d in (2, 1, 3):
        x_copy(1, d).start()
    x_own(0).start()
    x_own(1).start()
    loads[3].start()
    loads[4].start()

    loads[0].wait()

    def norm_rows(j, _):
        rs = pl.ds(pl.multiple_of(j * 64, 64), 64)
        r_ref[rs, :] = inv_rms(xv[rs, :], 1e-6)
        return 0

    lax.fori_loop(0, ROWS // 64, norm_rows, 0)
    loads[1].wait()
    loads[2].wait()

    steps = lax.dot_general(
        xv[...], ws[...], (((1,), (1,)), ((), ())), preferred_element_type=F32
    )
    steps = steps * r_ref[:, :H] + bias_ref[...]
    dt = jnp.maximum(steps, 0.0) + jnp.log(1.0 + jnp.exp(-jnp.abs(steps)))
    rate = rate_ref[...]
    row_id = lax.broadcasted_iota(jnp.int32, (CH, CH), 0)
    col_id = lax.broadcasted_iota(jnp.int32, (CH, CH), 1)
    causal = row_id >= col_id
    tri = jnp.where(causal, 1.0, 0.0).astype(F32)
    eye = jnp.where(row_id == col_id, 1.0, 0.0).astype(F32)
    offs = [jnp.zeros((1, H), F32)]
    ends = []
    fe = []
    for k in range(NCH):
        dt_k = dt[k * CH : (k + 1) * CH, :]
        a_k = -rate * dt_k
        la_k = jnp.dot(tri, a_k, precision=EXACT, preferred_element_type=F32)
        la_ref[k * CH : (k + 1) * CH, :] = la_k
        end_k = la_k[CH - 1 : CH, :]
        ends.append(end_k)
        off_ref[k, 0:1, 0:H] = offs[-1]
        offs.append(offs[-1] + end_k)
        fe.append(jnp.exp(end_k - la_k) * dt_k)
    ld_own[...] = jnp.zeros((8, 128), F32)
    ld_t[...] = jnp.zeros((8, 128), F32)
    ld_own[0:1, 0:H] = offs[NCH]

    def mix(j, _):
        cs = pl.ds(pl.multiple_of(j * MIX_T, MIX_T), MIX_T)
        part = jnp.dot(xv[...], wm[:, cs], preferred_element_type=F32)
        u[:, cs] = (part * widen(r_ref[...], MIX_T)).astype(BF)
        return 0

    lax.fori_loop(0, (D + 2 * N) // MIX_T, mix, 0)

    @pl.when(gateway)
    def _():
        pl.semaphore_wait(barrier, 20)
        for d in (1, 2, 3):
            pl.semaphore_signal(go_sem, inc=1, device_id=(t, ys[d]), device_id_type=MESH)

    for k in range(NCH):
        rs = pl.ds(k * CH, CH)
        scaled = (per_head(fe[k]) * u[rs, :D].astype(F32)).astype(BF)
        add = lax.dot_general(
            u[rs, D : D + N], scaled, (((0,), (0,)), ((), ())), preferred_element_type=F32
        )
        if k == 0:
            s_k[0] = jnp.zeros((N, D), BF)
            s_ref[...] = add
        else:
            s_k[k] = s_ref[...].astype(BF)
            s_ref[...] = s_ref[...] * per_head(jnp.exp(ends[k])) + add
    l_bf[...] = s_ref[...].astype(BF)

    loads[3].wait()

    def q_even(j, _):
        cs = pl.ds(pl.multiple_of(j * Q_T, Q_T), Q_T)
        rows = xv[...].reshape(4, 2, BLK, D)[:, 0].reshape(4 * BLK, D)
        scale = r_ref[...].reshape(4, 2, BLK, 128)[:, 0].reshape(4 * BLK, 128)
        part = jnp.dot(rows, wa[:, cs], preferred_element_type=F32) * widen(scale, Q_T)
        qe[:, :, cs] = head_scaled(part, 1e-6, mean_of).astype(BF).reshape(4, BLK, Q_T)
        return 0

    def q_copy(k):
        dev = (t_prev, 3) if k == 0 else (t, k - 1)
        return remote(
            qe.at[k], qt.at[1, pl.ds(pl.multiple_of(64 * y, 64), 64), :],
            q_ssem.at[k], q_rsem.at[y], dev,
        )

    def q_own(k):
        return pltpu.make_async_copy(
            qe.at[k], qt.at[1, pl.ds(pl.multiple_of(64 * y, 64), 64), :], q_rsem.at[y]
        )

    def diag(k, _):
        rs = pl.ds(pl.multiple_of(k * CH, CH), CH)
        cb = lax.dot_general(
            u[rs, D + N : D + 2 * N], u[rs, D : D + N], (((1,), (1,)), ((), ())),
            preferred_element_type=F32,
        )
        la_k = la_ref[rs, :]
        la_row = lat_t[k]
        dt_row = dt_t[k]
        for h in range(H):
            gap = la_k[:, h : h + 1] - la_row[h : h + 1, :]
            w = jnp.exp(jnp.where(causal, gap, -1e30)) * cb * dt_row[h : h + 1, :]
            yv[rs, h * HP : (h + 1) * HP] = jnp.dot(
                w.astype(BF), u[rs, h * HP : (h + 1) * HP], preferred_element_type=F32
            )
        return 0


    def attend_proj(i, width_from, dst, dst_from, tiles, scaled_tiles):
        def body(j, _):
            src = pl.ds(pl.multiple_of(width_from + j * KV_T, KV_T), KV_T)
            to = pl.ds(pl.multiple_of(dst_from + j * KV_T, KV_T), KV_T)
            part = jnp.dot(xt[i], wa[:, src], preferred_element_type=F32)
            part = part * widen(rt_ref[...], KV_T)
            if scaled_tiles:
                part = head_scaled(part, 1e-6, mean_of)
            dst[i, :, to] = part.astype(BF)
            return 0

        lax.fori_loop(0, tiles, body, 0)

    def norm_arriving(i):
        for d in (0, 1, 3, 2):
            if d == 0:
                x_own(i).wait()
            else:
                x_copy(i, d).wait_recv()
            rs = pl.ds(pl.multiple_of(64 * ys[(4 - d) % 4], 64), 64)
            rt_ref[rs, :] = inv_rms(xt[i, rs, :], 1e-6)

    half = pl.ds(pl.multiple_of(64 * core, 64), 64)
    other_half = pl.ds(pl.multiple_of(64 - 64 * core, 64), 64)
    a_copy = remote(l_bf.at[other_half, :], a_recv, a_ssem.at[0], a_rsem.at[0], mate)
    ld_copy = remote(ld_own, ld_a, a_ssem.at[1], a_rsem.at[1], mate)

    @pl.when(jnp.logical_not(gateway))
    def _():
        pl.semaphore_wait(go_sem, 1)

    ld_copy.start()
    a_copy.start()

    for k in range(NCH):
        dt_k = dt[k * CH : (k + 1) * CH, :]
        a_k = -rate * dt_k
        lat_t[k] = lax.dot_general(
            a_k, tri, (((0,), (1,)), ((), ())), precision=EXACT, preferred_element_type=F32
        )
        dt_t[k] = lax.dot_general(
            dt_k, eye, (((0,), (1,)), ((), ())), precision=EXACT, preferred_element_type=F32
        )


    a_copy.wait()
    ld_copy.wait()
    first = core == 0
    ld_mine = ld_own[0:1, 0:H]
    ld_theirs = ld_a[0:1, 0:H]
    ld0 = jnp.where(first, ld_mine, ld_theirs)
    ld1 = jnp.where(first, ld_theirs, ld_mine)
    ld_t[0:1, 0:H] = ld0 + ld1
    ld_b[chip] = ld_t[...]
    ld_copies = [remote(ld_t, ld_b.at[chip], b_ssem.at[1], b_rsem.at[1], chip_dev(i, j)) for i, j in plane]
    for cp in ld_copies:
        cp.start()

    mine = s_ref[half, :]
    theirs = a_recv[...].astype(F32)
    l0 = jnp.where(first, mine, theirs)
    l1 = jnp.where(first, theirs, mine)
    t_bf[...] = (per_head(jnp.exp(ld1)) * l0 + l1).astype(BF)

    def piece(ref, i, j):
        rows = pl.ds(pl.multiple_of(16 * j, 16), 16)
        lanes = pl.ds(pl.multiple_of(384 * i, 128), 384)
        return ref.at[rows, lanes]

    b_recv[chip] = t_bf[pl.ds(pl.multiple_of(16 * x, 16), 16), pl.ds(pl.multiple_of(384 * z, 128), 384)]
    for i, j in plane:
        remote(piece(t_bf, zs[i], xs[j]), b_recv.at[chip], b_ssem.at[0], b_rsem.at[0], chip_dev(i, j)).start()

    lax.fori_loop(0, AW // Q_T, q_even, 0)

    @pl.when(t > 0)
    def _():
        q_copy(0).start()

    for k in (1, 2, 3):

        @pl.when(y != k - 1)
        def _(k=k):
            q_copy(k).start()

        @pl.when(y == k - 1)
        def _(k=k):
            q_own(k).start()

    lax.fori_loop(0, 4, diag, 0)
    norm_arriving(0)
    attend_proj(0, AW, kv, 0, AW // KV_T, True)

    attend_proj(0, 2 * AW, kv, AW, AW // KV_T, False)

    def all_arrived(buf, ssem, rsem):
        part = buf.at[pl.ds(0, 15)]
        pltpu.make_async_copy(part, part, ssem).wait()
        pltpu.make_async_copy(part, part, rsem).wait()

    all_arrived(ld_b, b_ssem.at[1], b_rsem.at[1])
    all_arrived(b_recv, b_ssem.at[0], b_rsem.at[0])
    dec_ref[...] = per_head(jnp.exp(ld_b[:, 0, 0:H]))
    own_lanes = pl.ds(pl.multiple_of(384 * z, 128), 384)
    run = jnp.zeros((16, 384), F32)
    for j in range(16):
        d_send[j] = run.astype(BF)
        run = run * dec_ref[j : j + 1, own_lanes] + b_recv[j].astype(F32)
    own_rows = pl.ds(pl.multiple_of(16 * x, 16), 16)
    d_recv[own_rows, own_lanes] = d_send[chip]
    for i, j in plane:
        remote(
            d_send.at[zs[i] * 4 + xs[j]], piece(d_recv, z, x), d_ssem, d_rsem, chip_dev(i, j)
        ).start()

    norm_arriving(1)


    def q_odd(j, _):
        cs = pl.ds(pl.multiple_of(j * Q_T, Q_T), Q_T)
        part = jnp.dot(xt[1], wa[:, cs], preferred_element_type=F32) * widen(rt_ref[...], Q_T)
        qt[0, :, cs] = head_scaled(part, 1e-6, mean_of).astype(BF)
        return 0

    lax.fori_loop(0, AW // Q_T, q_odd, 0)

    def attention(i):
        for h in range(AH):
            hs = slice(h * HP, (h + 1) * HP)
            vs = slice(AW + h * HP, AW + (h + 1) * HP)
            s = lax.dot_general(
                qt[i, :, hs], kv[i, :, hs], (((1,), (1,)), ((), ())), preferred_element_type=F32
            )
            p = jnp.exp(s * (1.0 / math.sqrt(HP)))
            total = jnp.sum(p, axis=-1, keepdims=True)
            num = jnp.dot(p.astype(BF), kv[i, :, vs], preferred_element_type=F32)
            at_send[i, :, hs] = (num / total).astype(BF)

    def at_copy(i, d):
        src = at_send.at[i, pl.ds(pl.multiple_of(64 * ys[d], 64), 64), :]
        if i == 0:
            return remote(src, at_recv.at[1, y], at_ssem.at[i, d], at_rsem.at[1, y], (t, ys[d]))
        owner = jnp.where(last, t_next, t)
        k = ys[1]
        return remote(src, at_recv.at[0, k], at_ssem.at[i, d], at_rsem.at[0, k], (owner, ys[d]))

    def at_own(i):
        src = at_send.at[i, pl.ds(pl.multiple_of(64 * y, 64), 64), :]
        if i == 0:
            return pltpu.make_async_copy(src, at_recv.at[1, y], at_rsem.at[1, y])
        return pltpu.make_async_copy(src, at_recv.at[0, ys[1]], at_rsem.at[0, ys[1]])

    attention(0)
    for d in (2, 1, 3):
        at_copy(0, d).start()
    at_own(0).start()

    attend_proj(1, AW, kv, 0, AW // KV_T, True)
    attend_proj(1, 2 * AW, kv, AW, AW // KV_T, False)
    all_arrived(d_send, d_ssem, d_rsem)
    inc0 = d_recv[...].astype(F32)
    inc1 = per_head(jnp.exp(ld0)) * inc0 + l0
    e_send[...] = jnp.where(first, inc1, inc0).astype(BF)
    s_in[half, :] = jnp.where(first, inc0, inc1).astype(BF)
    e_copy = remote(e_send, s_in.at[half, :], e_ssem, e_rsem, mate)
    e_copy.start()

    @pl.when(followed)
    def _():
        for k in range(4):
            pltpu.make_async_copy(qe.at[k], qt.at[1, pl.ds(64 * k, 64), :], q_rsem.at[k]).wait()
        attention(1)
        for d in (2, 1, 3):
            at_copy(1, d).start()

    @pl.when(jnp.logical_and(last, followed))
    def _():
        at_copy(1, 0).start()

    @pl.when(jnp.logical_not(last))
    def _():
        at_own(1).start()

    e_copy.wait()


    def mixed(k, _):
        rs = pl.ds(pl.multiple_of(k * CH, CH), CH)
        c_k = u[rs, D + N : D + 2 * N]
        e_k = jnp.exp(la_ref[rs, :])
        e_in = jnp.exp(off_ref[k][0:1, 0:H])
        for h in range(0, H, 2):
            hs = slice(h * HP, (h + 2) * HP)
            state = s_k[k, :, hs].astype(F32) + pair(e_in, h) * s_in[:, hs].astype(F32)
            carried = jnp.dot(c_k, state.astype(BF), preferred_element_type=F32)
            m = yv[rs, hs] + pair(e_k, h) * carried
            ssm[rs, hs] = head_scaled(m, 1e-5, mean_of).astype(BF)
        return 0

    lax.fori_loop(0, NCH, mixed, 0)

    loads[4].wait()

    def out_ssm(j, _):
        cs = pl.ds(pl.multiple_of(j * OUT_T, OUT_T), OUT_T)
        part = jnp.dot(ssm[...], wo[:D, cs], preferred_element_type=F32)
        acc[:, :, :, cs] = (part + xv[:, cs].astype(F32)).reshape(4, 2, BLK, OUT_T)
        return 0

    lax.fori_loop(0, D // OUT_T, out_ssm, 0)

    for par in (1, 0):
        for k in range(4):
            arrival = pltpu.make_async_copy(
                at_send.at[0, pl.ds(0, 64), :], at_recv.at[par, k], at_rsem.at[par, k]
            )
            if par == 1 or k > 0:
                arrival.wait()
                continue

            @pl.when(t > 0)
            def _(arrival=arrival):
                arrival.wait()

            @pl.when(t == 0)
            def _():
                at_recv[0, 0] = jnp.zeros((BLK, AW), BF)

        def out_att(j, _, par=par):
            cs = pl.ds(pl.multiple_of(j * ATT_T, ATT_T), ATT_T)
            rows = at_recv[par].reshape(4 * BLK, AW)
            part = jnp.dot(rows, wo[D:, cs], preferred_element_type=F32)
            out_ref[:, par, :, cs] = (part.reshape(4, BLK, ATT_T) + acc[:, par, :, cs]).astype(BF)
            return 0

        lax.fori_loop(0, D // ATT_T, out_att, 0)

    for i in range(2):
        for d in (1, 2, 3):
            x_copy(i, d).wait_send()
    for d in (1, 2, 3):
        at_copy(0, d).wait_send()

    @pl.when(followed)
    def _():
        for d in (1, 2, 3):
            at_copy(1, d).wait_send()

    @pl.when(jnp.logical_and(last, followed))
    def _():
        at_copy(1, 0).wait_send()

    @pl.when(t > 0)
    def _():
        q_copy(0).wait_send()

    for k in (1, 2, 3):

        @pl.when(y != k - 1)
        def _(k=k):
            q_copy(k).wait_send()


def on_device(latents, mixer_weight, step_weight, step_bias, decay_rate, attend_weight, output_weight):
    any_spec = pl.BlockSpec(memory_space=pl.ANY)
    vmem_spec = pl.BlockSpec(memory_space=pltpu.VMEM)
    dma = pltpu.SemaphoreType.DMA
    v = pltpu.VMEM
    scratch = [
        v((ROWS, D), BF),
        v((2, POS, D), BF),
        v((D, D + 2 * N), BF),
        v((H, D), BF),
        v((D, 3 * AW), BF),
        v((D + AW, D), BF),
        v((ROWS, D + 2 * N), BF),
        v((ROWS, D), F32),
        v((4, 2, BLK, D), F32),
        v((ROWS, D), BF),
        v((2, POS, 2 * AW), BF),
        v((2, POS, AW), BF),
        v((4, BLK, AW), BF),
        v((2, POS, AW), BF),
        v((2, 4, BLK, AW), BF),
        v((ROWS, 128), F32),
        v((POS, 128), F32),
        v((ROWS, H), F32),
        v((NCH, 8, 128), F32),
        v((NCH, H, CH), F32),
        v((NCH, H, CH), F32),
        v((N, D), F32),
        v((NCH, N, D), BF),
        v((N, D), BF),
        v((64, D), BF),
        v((64, D), BF),
        v((16, 16, 384), BF),
        v((16, D), F32),
        v((16, 16, 384), BF),
        v((64, D), BF),
        v((64, D), BF),
        v((N, D), BF),
        v((8, 128), F32),
        v((8, 128), F32),
        v((8, 128), F32),
        v((16, 8, 128), F32),
        dma((13,)),
        dma((2,)),
        dma((2, 4)),
        dma((2, 4)),
        dma((4,)),
        dma((4,)),
        dma((2, 4)),
        dma((2, 4)),
        dma((2,)),
        dma((2,)),
        dma((2,)),
        dma((2,)),
        dma,
        dma,
        dma,
        dma,
        pltpu.SemaphoreType.REGULAR,
        pltpu.SemaphoreType.REGULAR,
    ]
    out = pl.pallas_call(
        kernel,
        out_shape=pltpu.VMEM((4, 2, BLK, D), BF),
        in_specs=[any_spec, any_spec, any_spec, vmem_spec, vmem_spec, any_spec, any_spec],
        out_specs=vmem_spec,
        scratch_shapes=scratch,
        compiler_params=pltpu.CompilerParams(
            collective_id=0, has_side_effects=True, vmem_limit_bytes=60 * 2**20
        ),
        cost_estimate=pl.CostEstimate(
            flops=12_000_000_000, bytes_accessed=24_000_000, transcendentals=4_000_000
        ),
    )(
        latents.reshape(ROWS, D),
        mixer_weight,
        step_weight.T,
        step_bias.reshape(1, H),
        decay_rate.reshape(1, H),
        attend_weight,
        output_weight,
    )
    return out.reshape(FR, BLK, D)


def solution(mesh):
    in_specs = (P("tm", "space", None), P(), P(), P(), P(), P(), P())
    out_specs = P("tm", "space", None)
    return jax.shard_map(
        on_device, mesh=mesh, in_specs=in_specs, out_specs=out_specs, check_vma=False
    )
```
